512 devices in a mesh: dp: 64 (over z, y_hi, core), tensor: 8 (over y_lo, x).
Axes of the slice: x: 4, y: 8 (y_hi: 4, y_lo: 2; y = y_hi * 2 + y_lo), z: 8, core: 2. Of those that a mesh axis runs over, the one named last changes fastest.
Arguments:
- activations: bfloat16 [8192, 8192], P('dp'), may hold values from -6 to 6
- norm_gain: bfloat16 [8192], replicated, may hold values from 0.099609375 to 1.8984375
- gate_w: bfloat16 [8192, 14336], P('dp', 'tensor'), may hold values from -0.0625 to 0.0625
- up_w: bfloat16 [8192, 14336], P('dp', 'tensor'), may hold values from -0.0625 to 0.0625
- down_w: bfloat16 [14336, 8192], P('tensor', 'dp'), may hold values from -0.1875 to 0.1875
- mask_gain: bfloat16 [14336], P('tensor'), may hold values from 0.29882812 to 3
- kept_blocks: int32 [8, 2], replicated, may hold values from 0 to 13, as said below
- kept_counts: int32 [8], replicated, may hold values from 0 to 2, as said below
- cotangent: bfloat16 [8192, 8192], P(('dp', 'tensor')), may hold values from -6 to 6
Outputs:
- input_grad: bfloat16 [8192, 8192], P(('dp', 'tensor'))
- gain_grad: float32 [16, 128], P('tensor', 'dp')
The draws below stay inside these ranges and needn't reach their ends.
Inputs may be any that keep to these rules, and one draw needn't show every extreme that they name: `kept_blocks`: in each row the first 2 entries are distinct; entries past the row's count are padding. `kept_counts`: the counts add up to 8; some shard has 2 and some has 0.
All inputs are finite; a program needn't handle non-finite values.
Results may differ from the reference program's by a relative error of at most 0.015.
Values may be sent and summed in bfloat16 or wider, within the bound.
No kernel may reach another device: no remote copies, remote signals or barrier semaphores. Data moves between devices by JAX's collectives and lax.ppermute only.
A program may use at most 64 MiB of HBM per device.

```python
import math
import jax
import jax.numpy as jnp
from jax import lax

D = 8192
FF = 14336
BLOCK = 128
KEEP = 2
TOKENS = 8192
BLK = 14
SLOTS = 16
N_TENSOR = 8


def draw_kept_blocks(key, part):
    key = jax.random.fold_in(key, 11)
    shards = SLOTS // KEEP
    keys = jax.random.split(key, shards + 3)
    rows = jax.vmap(lambda single: jax.random.permutation(single, BLK)[:KEEP])(keys[:shards]).astype(jnp.int32)
    row_pick = jax.random.randint(keys[shards], (), 0, shards).astype(jnp.int32)
    col_pick = jax.random.randint(keys[shards + 1], (), 0, KEEP).astype(jnp.int32)
    special = jax.random.permutation(keys[shards + 2], BLK - 1)[:KEEP].astype(jnp.int32)
    special = jnp.where(jnp.arange(KEEP, dtype=jnp.int32) == col_pick, BLK - 1, special).astype(jnp.int32)
    chosen = jnp.arange(shards, dtype=jnp.int32)[:, None] == row_pick
    return jnp.where(chosen, special[None, :], rows).astype(jnp.int32)


def draw_kept_counts(key, part):
    key = jax.random.fold_in(key, 12)
    shards = SLOTS // KEEP
    pairs = shards // 2
    first_key, rest_key, order_key = jax.random.split(key, 3)
    first = jax.random.randint(first_key, (1,), 0, 2) * KEEP
    rest = jax.random.randint(rest_key, (pairs - 1,), 0, KEEP + 1)
    leading = jnp.concatenate([first, rest]).astype(jnp.int32)
    flat = jnp.stack([leading, KEEP - leading], axis=1).reshape(-1)
    order = jax.random.permutation(order_key, shards)
    return flat[order].astype(jnp.int32)


def steps_of(key, dims, cuts, smallest, largest):
    def one(dim, shards_of):
        draws = jax.random.uniform(jax.random.fold_in(jax.random.fold_in(key, 6), dim), (shards_of,), jnp.float32, smallest / len(cuts), largest / len(cuts))
        return jnp.repeat(jnp.exp(draws), dims[dim] // shards_of).reshape((-1,) + (1,) * (len(dims) - dim - 1))

    gain = one(*cuts[0])
    for cut in cuts[1:]:
        gain = gain * one(*cut)
    return gain


def scatter_about(stream_key, extent, width, limit, pieces=(), kind=jnp.bfloat16):
    drawn = jax.random.normal(stream_key, extent, jnp.float32) * width
    if len(pieces) > 0:
        drawn = steps_of(stream_key, extent, pieces, -0.22, 0.18) * drawn
    return jnp.clip(drawn, min=-limit, max=limit).astype(kind)


def setup_inputs(seed: int = 0) -> dict:
    streams_of = jax.random.split(jax.random.key(seed), 10)
    return {
        "activations": scatter_about(streams_of[0], (TOKENS, D), 1.0, 6.0, ((0, 64),)),
        "norm_gain": jnp.clip(1.0 + 0.18 * jax.random.normal(streams_of[1], (D,), jnp.float32), 0.099609375, 1.8984375).astype(jnp.bfloat16),
        "gate_w": scatter_about(streams_of[2], (D, FF), D ** -0.5, 0.0625, ((0, 64), (1, 8))),
        "up_w": scatter_about(streams_of[3], (D, FF), D ** -0.5, 0.0625, ((0, 64), (1, 8))),
        "down_w": scatter_about(streams_of[4], (FF, D), (BLOCK * N_TENSOR) ** -0.5, 0.1875, ((0, 8), (1, 64))),
        "mask_gain": jnp.clip(jnp.exp(math.log(3.0) - 2.306499 * jax.random.uniform(streams_of[5], (FF,), jnp.float32) ** steps_of(streams_of[5], (FF,), ((0, 8),), -0.2, 0.2)), 0.29882812, 3.0).astype(jnp.bfloat16),
        "kept_blocks": draw_kept_blocks(jax.random.fold_in(streams_of[9], 71), 0),
        "kept_counts": draw_kept_counts(jax.random.fold_in(streams_of[9], 71), 0),
        "cotangent": scatter_about(streams_of[8], (TOKENS, D), 1.0, 6.0, ((0, 512),)),
    }


def reference(activations, norm_gain, gate_w, up_w, down_w, mask_gain, kept_blocks, kept_counts, cotangent):
    act_float = activations.astype(jnp.float32)
    inv_rms = lax.rsqrt(lax.optimization_barrier(jnp.mean(act_float * act_float, axis=-1, keepdims=True)) + 1e-05)
    normalized = act_float * inv_rms
    gain_float = norm_gain.astype(jnp.float32)
    normed = (normalized * gain_float).astype(jnp.bfloat16)
    scale = 1.0 / math.sqrt(TOKENS)
    dnormed = jnp.zeros((TOKENS, D), jnp.float32)
    grads = []
    units = jnp.arange(BLOCK, dtype=jnp.int32)
    slots = jnp.arange(KEEP, dtype=jnp.int32)
    for shard in range(N_TENSOR):
        blocks = kept_blocks[shard].astype(jnp.int32)
        index = ((shard * BLK + blocks)[:, None] * BLOCK + units[None, :]).reshape(-1)
        valid = jnp.repeat((slots < kept_counts[shard]).astype(jnp.float32), BLOCK)
        w_gate = jnp.take(gate_w, index, axis=1)
        w_up = jnp.take(up_w, index, axis=1)
        w_down = jnp.take(down_w, index, axis=0)
        gains = jnp.take(mask_gain, index).astype(jnp.float32) * valid
        gate = jnp.dot(normed, w_gate, preferred_element_type=jnp.float32)
        up = jnp.dot(normed, w_up, preferred_element_type=jnp.float32)
        sigmoid_gate = jax.nn.sigmoid(gate)
        activated = gate * sigmoid_gate * up
        hidden_grad = jnp.dot(cotangent, w_down.T, preferred_element_type=jnp.float32)
        grads.append((lax.optimization_barrier(jnp.sum(activated * hidden_grad, axis=0)) * scale * valid).reshape(KEEP, BLOCK))
        masked_grad = hidden_grad * gains
        gate_grad = (masked_grad * up * sigmoid_gate * (1.0 + gate * (1.0 - sigmoid_gate))).astype(jnp.bfloat16)
        up_grad = (masked_grad * gate * sigmoid_gate).astype(jnp.bfloat16)
        shard_part = jnp.dot(gate_grad, w_gate.T, preferred_element_type=jnp.float32)
        shard_part = shard_part + jnp.dot(up_grad, w_up.T, preferred_element_type=jnp.float32)
        dnormed = dnormed + shard_part.astype(jnp.bfloat16).astype(jnp.float32)
    scaled_grad = dnormed * gain_float
    input_grad = inv_rms * (scaled_grad - normalized * lax.optimization_barrier(jnp.mean(scaled_grad * normalized, axis=-1, keepdims=True)))
    return (input_grad.astype(jnp.bfloat16), jnp.concatenate(grads, axis=0))
```

```python
import functools
import math

import jax
import jax.numpy as jnp
from jax import lax
from jax.experimental import pallas as pl
from jax.experimental.pallas import tpu as pltpu
from jax.sharding import Mesh
from jax.sharding import PartitionSpec as P

BLOCK = 128
Z, YH, CORE, YL, X = 8, 4, 2, 2, 4
DP = ("z", "yh", "core")
TENSOR = ("yl", "x")
SHARDS = YL * X
BF, F32 = jnp.bfloat16, jnp.float32
EXTRA = 16
NT = (((1,), (1,)), ((), ()))


def first_slot(counts_ref, shard):
    total = jnp.int32(0)
    for other in range(SHARDS):
        total += jnp.where(other < shard, counts_ref[other], 0)
    return total


def pack_kernel(place, kept, counts, g0, g1, u0, u1, d0, d1, m0, m1, out):
    first = first_slot(counts, place[0])
    slots = []
    for gate, up, down, gain in ((g0, u0, d0, m0), (g1, u1, d1, m1)):
        body = jnp.concatenate([gate[...], up[...], down[...].T], axis=1)
        row = jnp.broadcast_to(gain[0], (EXTRA, BLOCK))
        slots.append((body, jnp.concatenate([row] * 3, axis=1)))
    for dest in range(SHARDS):
        second = dest == first + 1
        out[dest, :BLOCK, :] = jnp.where(second, slots[1][0], slots[0][0])
        out[dest, BLOCK:, :] = jnp.where(second, slots[1][1], slots[0][1])


def pack(place, kept, counts, gate_w, up_w, down_w, mask_gain):
    rows, units = gate_w.shape
    blocks = units // BLOCK

    def pick(k, kept, place):
        return jnp.clip(kept[place[0], k], 0, blocks - 1)

    cols = [
        pl.BlockSpec((rows, BLOCK), lambda i, p, b, n, k=k: (0, pick(k, b, p)))
        for k in (0, 1)
    ]
    down = [
        pl.BlockSpec((BLOCK, rows), lambda i, p, b, n, k=k: (pick(k, b, p), 0))
        for k in (0, 1)
    ]
    gain = [
        pl.BlockSpec((1, 1, BLOCK), lambda i, p, b, n, k=k: (pick(k, b, p), 0, 0))
        for k in (0, 1)
    ]
    gains = mask_gain.reshape(blocks, 1, BLOCK)
    shape = (SHARDS, BLOCK + EXTRA, 3 * BLOCK)
    return pl.pallas_call(
        pack_kernel,
        out_shape=jax.ShapeDtypeStruct(shape, BF),
        grid_spec=pltpu.PrefetchScalarGridSpec(
            num_scalar_prefetch=3,
            grid=(1,),
            in_specs=cols + cols + down + gain,
            out_specs=pl.BlockSpec(shape, lambda i, *_: (0, 0, 0)),
        ),
        name="pack_slots",
    )(place, kept, counts, gate_w, gate_w, up_w, up_w, down_w, down_w, gains, gains)


def ffn_kernel(scale, place, normed, cot, gain, *refs):
    nchunk = (len(refs) - 1) // 2
    mine, theirs, out = refs[:nchunk], refs[nchunk : 2 * nchunk], refs[-1]
    z, core = place[1], place[2]
    pieces = [(z, 0)]
    for step in (1, 2, 3):
        pieces += [(lax.rem(z - step + Z, Z), 0), (lax.rem(z + step, Z), 0)]
    far = lax.rem(z + Z // 2, Z)
    pieces += [(far, 0), (far, YH // 2)]
    work = []
    for (zz, yh0), a, b in zip(pieces, mine, theirs):
        for k in range(a.shape[0] // BLOCK):
            at = (zz * YH + yh0 + k) * (CORE * BLOCK)
            near = pl.multiple_of(at + core * BLOCK, BLOCK)
            other = pl.multiple_of(at + (1 - core) * BLOCK, BLOCK)
            work.append((near, other, a, b, k * BLOCK))
    tokens = normed.shape[0]
    gate_up = jnp.zeros((tokens, 2 * BLOCK), F32)
    hidden = jnp.zeros((tokens, BLOCK), F32)
    for near, other, a, b, row in work:
        n2 = jnp.concatenate([normed[:, pl.ds(near, BLOCK)], normed[:, pl.ds(other, BLOCK)]], axis=1)
        c2 = jnp.concatenate([cot[:, pl.ds(near, BLOCK)], cot[:, pl.ds(other, BLOCK)]], axis=1)
        w2 = jnp.concatenate([a[row : row + BLOCK, :], b[row : row + BLOCK, :]], axis=0)
        gate_up += jnp.dot(n2, w2[:, : 2 * BLOCK], preferred_element_type=F32)
        hidden += jnp.dot(c2, w2[:, 2 * BLOCK :], preferred_element_type=F32)
    gate, up = gate_up[:, :BLOCK], gate_up[:, BLOCK:]
    sig = jax.nn.sigmoid(gate)
    unit = jnp.sum(gate * sig * up * hidden, axis=0, keepdims=True) * scale
    masked = hidden * gain[0:1, :].astype(F32)
    gate_grad = (masked * up * sig * (1.0 + gate * (1.0 - sig))).astype(BF)
    up_grad = (masked * gate * sig).astype(BF)
    grads = jnp.concatenate([gate_grad, up_grad], axis=1)
    share = tokens // SHARDS
    for near, other, a, b, row in work:
        for at, w in ((near, a), (other, b)):
            part = lax.dot_general(grads, w[row : row + BLOCK, : 2 * BLOCK], NT, preferred_element_type=F32)
            first = pl.multiple_of(at // BLOCK * share, share)
            out[:, pl.ds(first, share), :] = part.astype(BF).reshape(SHARDS, share, BLOCK)
    hi = unit.astype(BF)
    rest = unit - hi.astype(F32)
    mid = rest.astype(BF)
    lo = (rest - mid.astype(F32)).astype(BF)
    row = lax.broadcasted_iota(jnp.int32, (EXTRA, BLOCK), 0)
    split = jnp.where(
        row == 0, hi.astype(F32), jnp.where(row == 1, mid.astype(F32), jnp.where(row == 2, lo.astype(F32), 0.0))
    ).astype(BF)
    for dest in range(SHARDS):
        out[dest, -EXTRA:, :] = split


def ffn(place, normed, cot, gain, mine, theirs):
    tokens, width = normed.shape
    rows = width // BLOCK * (tokens // SHARDS) + EXTRA
    vmem = pl.BlockSpec(memory_space=pltpu.VMEM)
    scale = 1.0 / math.sqrt(tokens * Z * YH * CORE)
    return pl.pallas_call(
        functools.partial(ffn_kernel, scale),
        out_shape=jax.ShapeDtypeStruct((SHARDS, rows, BLOCK), BF),
        in_specs=[pl.BlockSpec(memory_space=pltpu.SMEM)] + [vmem] * (3 + len(mine) + len(theirs)),
        out_specs=vmem,
        compiler_params=pltpu.CompilerParams(vmem_limit_bytes=48 << 20),
        name="pruned_ffn",
    )(place, normed, cot, gain, *mine, *theirs)


def final_kernel(place, counts, act, gain, parts, grad, unit):
    share, width = act.shape
    x = act[...].astype(F32)
    inv = lax.rsqrt(jnp.mean(x * x, axis=-1, keepdims=True) + 1e-05)
    dnormed = []
    for j in range(width // BLOCK):
        total = parts[0, j * share : (j + 1) * share, :].astype(F32)
        for src in range(1, SHARDS):
            total += parts[src, j * share : (j + 1) * share, :].astype(F32)
        dnormed.append(total)
    scaled = jnp.concatenate(dnormed, axis=1) * gain[...].astype(F32)
    normalized = x * inv
    mean = jnp.mean(scaled * normalized, axis=-1, keepdims=True)
    grad[...] = (inv * (scaled - normalized * mean)).astype(BF)
    me = place[0]
    first, count = first_slot(counts, me), counts[me]
    for k in range(2):
        tail = parts[jnp.minimum(first + k, SHARDS - 1), -EXTRA:, :].astype(F32)
        value = jnp.sum(tail, axis=0, keepdims=True)
        unit[k : k + 1, :] = jnp.where(k < count, value, 0.0)


def final(place, counts, act, gain, parts):
    tokens, width = act.shape
    share = tokens // SHARDS
    return pl.pallas_call(
        final_kernel,
        out_shape=(
            jax.ShapeDtypeStruct((share, width), BF),
            jax.ShapeDtypeStruct((2, BLOCK), F32),
        ),
        grid_spec=pltpu.PrefetchScalarGridSpec(
            num_scalar_prefetch=2,
            grid=(1,),
            in_specs=[
                pl.BlockSpec((share, width), lambda i, p, n: (p[0], 0)),
                pl.BlockSpec((1, width), lambda i, p, n: (0, 0)),
                pl.BlockSpec(parts.shape, lambda i, p, n: (0, 0, 0)),
            ],
            out_specs=(
                pl.BlockSpec((share, width), lambda i, p, n: (0, 0)),
                pl.BlockSpec((2, BLOCK), lambda i, p, n: (0, 0)),
            ),
        ),
        compiler_params=pltpu.CompilerParams(vmem_limit_bytes=32 << 20),
        name="input_grad",
    )(place, counts, act, gain.reshape(1, -1), parts)


def ring(x):
    up = [(i, (i + 1) % Z) for i in range(Z)]
    down = [(i, (i - 1) % Z) for i in range(Z)]
    chunks, a, b = [x], x, x
    for _ in range(3):
        a, b = lax.ppermute(a, "z", up), lax.ppermute(b, "z", down)
        chunks += [a, b]
    half = x.shape[0] // 2
    chunks += [lax.ppermute(a[:half], "z", up), lax.ppermute(b[half:], "z", down)]
    return chunks


def per_device(
    activations, norm_gain, gate_w, up_w, down_w, mask_gain, kept_blocks, kept_counts, cotangent
):
    me = lax.axis_index(TENSOR)
    place = jnp.stack([me, lax.axis_index("z"), lax.axis_index("core")]).astype(jnp.int32)
    cot = lax.all_gather(cotangent, TENSOR, axis=0, tiled=True)

    sent = pack(place, kept_blocks, kept_counts, gate_w, up_w, down_w, mask_gain)
    got = lax.all_to_all(sent, TENSOR, split_axis=0, concat_axis=0, tiled=True)
    ends = jnp.cumsum(kept_counts)
    source = jnp.sum((ends <= me).astype(jnp.int32))
    slot = lax.dynamic_index_in_dim(got, source, 0, keepdims=False)
    unit_gain = slot[BLOCK:, :BLOCK]
    column = lax.all_gather(slot[:BLOCK], "yh", axis=0, tiled=True)
    mine = ring(column)
    swap = [(0, 1), (1, 0)]
    theirs = [lax.ppermute(chunk, "core", swap) for chunk in mine]

    act = activations.astype(F32)
    inv_rms = lax.rsqrt(jnp.mean(act * act, axis=-1, keepdims=True) + 1e-05)
    normed = (act * inv_rms * norm_gain.astype(F32)).astype(BF)

    parts = ffn(place, normed, cot, unit_gain, mine, theirs)
    got = lax.all_to_all(parts, TENSOR, split_axis=0, concat_axis=0, tiled=True)
    input_grad, unit = final(place, kept_counts, activations, norm_gain, got)
    copies = jnp.broadcast_to(unit[None], (Z * YH * CORE, 2, BLOCK))
    units = jnp.sum(lax.all_to_all(copies, DP, split_axis=0, concat_axis=0, tiled=True), axis=0)
    width = BLOCK // (Z * YH * CORE)
    gain_grad = lax.dynamic_slice_in_dim(units, lax.axis_index(DP) * width, width, 1)
    return input_grad, gain_grad


def solution(mesh):
    fine = Mesh(mesh.devices.reshape(Z, YH, CORE, YL, X), DP + TENSOR)
    placed = (
        P(DP, None),
        P(),
        P(DP, TENSOR),
        P(DP, TENSOR),
        P(TENSOR, DP),
        P(TENSOR),
        P(),
        P(),
        P(DP + TENSOR, None),
    )
    return jax.shard_map(
        per_device,
        mesh=fine,
        in_specs=placed,
        out_specs=(P(DP + TENSOR, None), P(TENSOR, DP)),
        check_vma=False,
    )
```

```python
import functools
import math

import jax
import jax.numpy as jnp
from jax import lax
from jax.experimental import pallas as pl
from jax.experimental.pallas import tpu as pltpu
from jax.sharding import Mesh
from jax.sharding import PartitionSpec as P

BLOCK = 128
Z, YH, CORE, YL, X = 8, 4, 2, 2, 4
DP = ("z", "yh", "core")
TENSOR = ("yl", "x")
SHARDS = YL * X
BF, F32 = jnp.bfloat16, jnp.float32
EXTRA = 16
UNITS = (8,)
NT = (((1,), (1,)), ((), ()))


def first_slot(counts_ref, shard):
    total = jnp.int32(0)
    for other in range(SHARDS):
        total += jnp.where(other < shard, counts_ref[other], 0)
    return total


def pack_kernel(place, kept, counts, g0, g1, u0, u1, d0, d1, m0, m1, out):
    first = first_slot(counts, place[0])
    slots = []
    for gate, up, down, gain in ((g0, u0, d0, m0), (g1, u1, d1, m1)):
        body = jnp.concatenate([gate[...], up[...], down[...].T], axis=1)
        row = jnp.broadcast_to(gain[0], (EXTRA, BLOCK))
        slots.append((body, jnp.concatenate([row] * 3, axis=1)))
    for dest in range(SHARDS):
        second = dest == first + 1
        out[dest, :BLOCK, :] = jnp.where(second, slots[1][0], slots[0][0])
        out[dest, BLOCK:, :] = jnp.where(second, slots[1][1], slots[0][1])


def pack(place, kept, counts, gate_w, up_w, down_w, mask_gain):
    rows, units = gate_w.shape
    blocks = units // BLOCK

    def pick(k, kept, place):
        return jnp.clip(kept[place[0], k], 0, blocks - 1)

    cols = [
        pl.BlockSpec((rows, BLOCK), lambda i, p, b, n, k=k: (0, pick(k, b, p)))
        for k in (0, 1)
    ]
    down = [
        pl.BlockSpec((BLOCK, rows), lambda i, p, b, n, k=k: (pick(k, b, p), 0))
        for k in (0, 1)
    ]
    gain = [
        pl.BlockSpec((1, 1, BLOCK), lambda i, p, b, n, k=k: (pick(k, b, p), 0, 0))
        for k in (0, 1)
    ]
    gains = mask_gain.reshape(blocks, 1, BLOCK)
    shape = (SHARDS, BLOCK + EXTRA, 3 * BLOCK)
    return pl.pallas_call(
        pack_kernel,
        out_shape=jax.ShapeDtypeStruct(shape, BF),
        grid_spec=pltpu.PrefetchScalarGridSpec(
            num_scalar_prefetch=3,
            grid=(1,),
            in_specs=cols + cols + down + gain,
            out_specs=pl.BlockSpec(shape, lambda i, *_: (0, 0, 0)),
        ),
        name="pack_slots",
    )(place, kept, counts, gate_w, gate_w, up_w, up_w, down_w, down_w, gains, gains)


def ffn_kernel(scale, layout, place, normed, cot, gain, *refs):
    count = len(layout)
    mine, theirs = refs[:count], refs[count : 2 * count]
    out, unit_out = refs[2 * count : 2 * count + 2]
    n_buf, c_buf = refs[2 * count + 2 : 2 * count + 4]
    a_buf, b_buf = refs[2 * count + 4 : 3 * count + 4], refs[3 * count + 4 : 4 * count + 4]
    sems = refs[-1]
    z, core = place[1], place[2]
    copies, work = [], []

    def copy(source, target):
        one = pltpu.make_async_copy(source, target, sems.at[len(copies)])
        one.start()
        copies.append(one)
        return one

    half = normed.shape[1] // 2
    acts = []
    for source, target in ((normed, n_buf), (cot, c_buf)):
        for k in range(2):
            cols = pl.ds(k * half, half)
            acts.append(copy(source.at[:, cols], target.at[:, cols]))
    for i, pieces in enumerate(layout):
        row = 0
        for shift, yh0, length in pieces:
            rows = pl.ds(row, length * BLOCK)
            both = [
                copy(mine[i].at[rows, :], a_buf[i].at[rows, :]),
                copy(theirs[i].at[rows, :], b_buf[i].at[rows, :]),
            ]
            zz = shift[0] if isinstance(shift, tuple) else lax.rem(z + shift + Z, Z)
            for k in range(length):
                at = (zz * YH + yh0 + k) * (CORE * BLOCK)
                near = pl.multiple_of(at + core * BLOCK, BLOCK)
                other = pl.multiple_of(at + (1 - core) * BLOCK, BLOCK)
                work.append((both if k == 0 else [], near, other, a_buf[i], b_buf[i], row))
                row += BLOCK
    for one in acts:
        one.wait()
    tokens = normed.shape[0]
    gate_up = jnp.zeros((tokens, 2 * BLOCK), F32)
    hidden = jnp.zeros((tokens, BLOCK), F32)
    for waits, near, other, a, b, row in work:
        for one in waits:
            one.wait()
        n2 = jnp.concatenate([n_buf[:, pl.ds(near, BLOCK)], n_buf[:, pl.ds(other, BLOCK)]], axis=1)
        c2 = jnp.concatenate([c_buf[:, pl.ds(near, BLOCK)], c_buf[:, pl.ds(other, BLOCK)]], axis=1)
        w2 = jnp.concatenate([a[row : row + BLOCK, :], b[row : row + BLOCK, :]], axis=0)
        gate_up += jnp.dot(n2, w2[:, : 2 * BLOCK], preferred_element_type=F32)
        hidden += jnp.dot(c2, w2[:, 2 * BLOCK :], preferred_element_type=F32)
    gate, up = gate_up[:, :BLOCK], gate_up[:, BLOCK:]
    sig = jax.nn.sigmoid(gate)
    unit = jnp.sum(gate * sig * up * hidden, axis=0, keepdims=True) * scale
    unit_out[...] = jnp.broadcast_to(unit, unit_out.shape)
    masked = hidden * gain[0:1, :].astype(F32)
    gate_grad = (masked * up * sig * (1.0 + gate * (1.0 - sig))).astype(BF)
    up_grad = (masked * gate * sig).astype(BF)
    grads = jnp.concatenate([gate_grad, up_grad], axis=1)
    share = tokens // SHARDS
    for _, near, other, a, b, row in work:
        for at, w in ((near, a), (other, b)):
            part = lax.dot_general(grads, w[row : row + BLOCK, : 2 * BLOCK], NT, preferred_element_type=F32)
            first = pl.multiple_of(at // BLOCK * share, share)
            out[:, pl.ds(first, share), :] = part.astype(BF).reshape(SHARDS, share, BLOCK)


def ffn(place, normed, cot, gain, layout, mine, theirs):
    tokens, width = normed.shape
    rows = width // BLOCK * (tokens // SHARDS)
    vmem = pl.BlockSpec(memory_space=pltpu.VMEM)
    anyw = pl.BlockSpec(memory_space=pl.ANY)
    scale = 1.0 / math.sqrt(tokens * Z * YH * CORE)
    buffers = [pltpu.VMEM(x.shape, BF) for x in (normed, cot, *mine, *theirs)]
    copies = 4 + 2 * sum(len(pieces) for pieces in layout)
    return pl.pallas_call(
        functools.partial(ffn_kernel, scale, layout),
        out_shape=(
            jax.ShapeDtypeStruct((SHARDS, rows, BLOCK), BF),
            jax.ShapeDtypeStruct(UNITS + (BLOCK,), F32),
        ),
        in_specs=[pl.BlockSpec(memory_space=pltpu.SMEM), anyw, anyw, vmem] + [anyw] * (2 * len(mine)),
        out_specs=(vmem, vmem),
        scratch_shapes=buffers + [pltpu.SemaphoreType.DMA((copies,))],
        compiler_params=pltpu.CompilerParams(vmem_limit_bytes=56 << 20),
        name="pruned_ffn",
    )(place, normed, cot, gain, *mine, *theirs)


def final_kernel(place, act, gain, parts, grad):
    share, width = act.shape
    x = act[...].astype(F32)
    inv = lax.rsqrt(jnp.mean(x * x, axis=-1, keepdims=True) + 1e-05)
    dnormed = []
    for j in range(width // BLOCK):
        total = parts[0, j * share : (j + 1) * share, :].astype(F32)
        for src in range(1, SHARDS):
            total += parts[src, j * share : (j + 1) * share, :].astype(F32)
        dnormed.append(total)
    scaled = jnp.concatenate(dnormed, axis=1) * gain[...].astype(F32)
    normalized = x * inv
    mean = jnp.mean(scaled * normalized, axis=-1, keepdims=True)
    grad[...] = (inv * (scaled - normalized * mean)).astype(BF)


def final(place, act, gain, parts):
    tokens, width = act.shape
    share = tokens // SHARDS
    return pl.pallas_call(
        final_kernel,
        out_shape=jax.ShapeDtypeStruct((share, width), BF),
        grid_spec=pltpu.PrefetchScalarGridSpec(
            num_scalar_prefetch=1,
            grid=(1,),
            in_specs=[
                pl.BlockSpec((share, width), lambda i, p: (p[0], 0)),
                pl.BlockSpec((1, width), lambda i, p: (0, 0)),
                pl.BlockSpec(parts.shape, lambda i, p: (0, 0, 0)),
            ],
            out_specs=pl.BlockSpec((share, width), lambda i, p: (0, 0)),
        ),
        compiler_params=pltpu.CompilerParams(vmem_limit_bytes=12 << 20),
        name="input_grad",
    )(place, act, gain.reshape(1, -1), parts)


def whole(x, yh0):
    length = x.shape[0] // BLOCK
    return lax.all_gather(x, "z", axis=0, tiled=True), tuple(((i,), yh0, length) for i in range(Z))


def swapped(x, axis, size, distance):
    return lax.ppermute(x, axis, [(i, i ^ distance) for i in range(size)])


def summed_over_dp(x):
    for axis, size in (("core", CORE), ("yh", YH), ("z", Z)):
        distance = 1
        while distance < size:
            x = x + swapped(x, axis, size, distance)
            distance *= 2
    return x


def per_device(
    activations, norm_gain, gate_w, up_w, down_w, mask_gain, kept_blocks, kept_counts, cotangent
):
    me = lax.axis_index(TENSOR)
    place = jnp.stack([me, lax.axis_index("z"), lax.axis_index("core")]).astype(jnp.int32)

    sent = pack(place, kept_blocks, kept_counts, gate_w, up_w, down_w, mask_gain)
    got = lax.all_to_all(sent, TENSOR, split_axis=0, concat_axis=0, tiled=True)
    ends = jnp.cumsum(kept_counts)
    source = jnp.sum((ends <= me).astype(jnp.int32))
    slot = lax.dynamic_index_in_dim(got, source, 0, keepdims=False)
    column = lax.all_gather(slot[:BLOCK], "yh", axis=0, tiled=True)
    weights, order = whole(column, 0)

    cotangent, activations_late, slot, _ = lax.optimization_barrier((cotangent, activations, slot, column))
    unit_gain = slot[BLOCK:, :BLOCK]
    wide = jnp.broadcast_to(cotangent[None], (SHARDS,) + cotangent.shape)
    cot = lax.all_to_all(wide, TENSOR, split_axis=0, concat_axis=0, tiled=True).reshape(-1, cotangent.shape[1])
    act = activations_late.astype(F32)
    inv_rms = lax.rsqrt(jnp.mean(act * act, axis=-1, keepdims=True) + 1e-05)
    normed = (act * inv_rms * norm_gain.astype(F32)).astype(BF)

    other = lax.ppermute(weights, "core", [(0, 1), (1, 0)])
    parts, unit = ffn(place, normed, cot, unit_gain, (order,), [weights], [other])
    got = lax.all_to_all(parts, TENSOR, split_axis=0, concat_axis=0, tiled=True)
    input_grad = final(place, activations, norm_gain, got)

    units = lax.all_gather(summed_over_dp(unit)[:1], TENSOR, axis=0, tiled=True)
    width = BLOCK // (Z * YH * CORE)
    count = kept_counts[me]
    slots = ends[me] - count + jnp.arange(2)
    mine_units = lax.dynamic_slice_in_dim(units, lax.axis_index(DP) * width, width, 1)
    picked = jnp.take(mine_units, jnp.minimum(slots, SHARDS - 1), axis=0)
    gain_grad = jnp.where((jnp.arange(2) < count)[:, None], picked, 0.0)
    return input_grad, gain_grad


def solution(mesh):
    fine = Mesh(mesh.devices.reshape(Z, YH, CORE, YL, X), DP + TENSOR)
    placed = (
        P(DP, None),
        P(),
        P(DP, TENSOR),
        P(DP, TENSOR),
        P(TENSOR, DP),
        P(TENSOR),
        P(),
        P(),
        P(DP + TENSOR, None),
    )
    return jax.shard_map(
        per_device,
        mesh=fine,
        in_specs=placed,
        out_specs=(P(DP + TENSOR, None), P(TENSOR, DP)),
        check_vma=False,
    )
```

```python
import functools
import math

import jax
import jax.numpy as jnp
from jax import lax
from jax.experimental import pallas as pl
from jax.experimental.pallas import tpu as pltpu
from jax.sharding import Mesh
from jax.sharding import PartitionSpec as P

BLOCK = 128
Z, YH, CORE, YL, X = 8, 4, 2, 2, 4
DP = ("z", "yh", "core")
TENSOR = ("yl", "x")
SHARDS = YL * X
BF, F32 = jnp.bfloat16, jnp.float32
EXTRA = 16
UNITS = (8,)
PARTS = 2
NT = (((1,), (1,)), ((), ()))


def first_slot(counts_ref, shard):
    total = jnp.int32(0)
    for other in range(SHARDS):
        total += jnp.where(other < shard, counts_ref[other], 0)
    return total


def pack_kernel(place, kept, counts, g0, g1, u0, u1, d0, d1, m0, m1, out):
    first = first_slot(counts, place[0])
    slots = []
    for gate, up, down, gain in ((g0, u0, d0, m0), (g1, u1, d1, m1)):
        body = jnp.concatenate([gate[...], up[...], down[...].T], axis=1)
        row = jnp.broadcast_to(gain[0], (EXTRA, BLOCK))
        slots.append((body, jnp.concatenate([row] * 3, axis=1)))
    for dest in range(SHARDS):
        second = dest == first + 1
        out[dest, :BLOCK, :] = jnp.where(second, slots[1][0], slots[0][0])
        out[dest, BLOCK:, :] = jnp.where(second, slots[1][1], slots[0][1])


def pack(place, kept, counts, gate_w, up_w, down_w, mask_gain):
    rows, units = gate_w.shape
    blocks = units // BLOCK

    def pick(k, kept, place):
        return jnp.clip(kept[place[0], k], 0, blocks - 1)

    cols = [
        pl.BlockSpec((rows, BLOCK), lambda i, p, b, n, k=k: (0, pick(k, b, p)))
        for k in (0, 1)
    ]
    down = [
        pl.BlockSpec((BLOCK, rows), lambda i, p, b, n, k=k: (pick(k, b, p), 0))
        for k in (0, 1)
    ]
    gain = [
        pl.BlockSpec((1, 1, BLOCK), lambda i, p, b, n, k=k: (pick(k, b, p), 0, 0))
        for k in (0, 1)
    ]
    gains = mask_gain.reshape(blocks, 1, BLOCK)
    shape = (SHARDS, BLOCK + EXTRA, 3 * BLOCK)
    return pl.pallas_call(
        pack_kernel,
        out_shape=jax.ShapeDtypeStruct(shape, BF),
        grid_spec=pltpu.PrefetchScalarGridSpec(
            num_scalar_prefetch=3,
            grid=(1,),
            in_specs=cols + cols + down + gain,
            out_specs=pl.BlockSpec(shape, lambda i, *_: (0, 0, 0)),
        ),
        name="pack_slots",
    )(place, kept, counts, gate_w, gate_w, up_w, up_w, down_w, down_w, gains, gains)


def ffn_kernel(scale, layout, place, normed, cot, gain, *refs):
    count = len(layout)
    mine, theirs = refs[:count], refs[count : 2 * count]
    out, unit_out = refs[2 * count : 2 * count + 2]
    n_buf, c_buf = refs[2 * count + 2 : 2 * count + 4]
    a_buf, b_buf = refs[2 * count + 4 : 3 * count + 4], refs[3 * count + 4 : 4 * count + 4]
    sems = refs[-1]
    z, core = place[1], place[2]
    copies, work = [], []

    def copy(source, target):
        one = pltpu.make_async_copy(source, target, sems.at[len(copies)])
        one.start()
        copies.append(one)
        return one

    half = normed.shape[1] // 2
    acts = []
    for source, target in ((normed, n_buf), (cot, c_buf)):
        for k in range(2):
            cols = pl.ds(k * half, half)
            acts.append(copy(source.at[:, cols], target.at[:, cols]))
    for i, pieces in enumerate(layout):
        row = 0
        for shift, yh0, length in pieces:
            rows = pl.ds(row, length * BLOCK)
            both = [
                copy(mine[i].at[rows, :], a_buf[i].at[rows, :]),
                copy(theirs[i].at[rows, :], b_buf[i].at[rows, :]),
            ]
            zz = shift[0] if isinstance(shift, tuple) else lax.rem(z + shift + Z, Z)
            for k in range(length):
                at = (zz * YH + lax.rem(place[3] - yh0 - k + YH, YH)) * (CORE * BLOCK)
                near = pl.multiple_of(at + core * BLOCK, BLOCK)
                other = pl.multiple_of(at + (1 - core) * BLOCK, BLOCK)
                work.append((both if k == 0 else [], near, other, a_buf[i], b_buf[i], row))
                row += BLOCK
    for one in acts:
        one.wait()
    tokens = normed.shape[0]
    gate_up = jnp.zeros((tokens, 2 * BLOCK), F32)
    hidden = jnp.zeros((tokens, BLOCK), F32)
    for waits, near, other, a, b, row in work:
        for one in waits:
            one.wait()
        n2 = jnp.concatenate([n_buf[:, pl.ds(near, BLOCK)], n_buf[:, pl.ds(other, BLOCK)]], axis=1)
        c2 = jnp.concatenate([c_buf[:, pl.ds(near, BLOCK)], c_buf[:, pl.ds(other, BLOCK)]], axis=1)
        w2 = jnp.concatenate([a[row : row + BLOCK, :], b[row : row + BLOCK, :]], axis=0)
        gate_up += jnp.dot(n2, w2[:, : 2 * BLOCK], preferred_element_type=F32)
        hidden += jnp.dot(c2, w2[:, 2 * BLOCK :], preferred_element_type=F32)
    gate, up = gate_up[:, :BLOCK], gate_up[:, BLOCK:]
    sig = jax.nn.sigmoid(gate)
    unit = jnp.sum(gate * sig * up * hidden, axis=0, keepdims=True) * scale
    unit_out[...] = jnp.broadcast_to(unit, unit_out.shape)
    masked = hidden * gain[0:1, :].astype(F32)
    gate_grad = (masked * up * sig * (1.0 + gate * (1.0 - sig))).astype(BF)
    up_grad = (masked * gate * sig).astype(BF)
    grads = jnp.concatenate([gate_grad, up_grad], axis=1)
    share = tokens // SHARDS
    for _, near, other, a, b, row in work:
        for at, w in ((near, a), (other, b)):
            part = lax.dot_general(grads, w[row : row + BLOCK, : 2 * BLOCK], NT, preferred_element_type=F32)
            first = pl.multiple_of(at // BLOCK * share, share)
            out[:, pl.ds(first, share), :] = part.astype(BF).reshape(SHARDS, share, BLOCK)


def ffn(place, normed, cot, gain, layout, mine, theirs):
    tokens, width = normed.shape
    rows = width // BLOCK * (tokens // SHARDS)
    vmem = pl.BlockSpec(memory_space=pltpu.VMEM)
    anyw = pl.BlockSpec(memory_space=pl.ANY)
    scale = 1.0 / math.sqrt(tokens * Z * YH * CORE)
    buffers = [pltpu.VMEM(x.shape, BF) for x in (normed, cot, *mine, *theirs)]
    copies = 4 + 2 * sum(len(pieces) for pieces in layout)
    return pl.pallas_call(
        functools.partial(ffn_kernel, scale, layout),
        out_shape=(
            jax.ShapeDtypeStruct((SHARDS, rows, BLOCK), BF),
            jax.ShapeDtypeStruct(UNITS + (BLOCK,), F32),
        ),
        in_specs=[pl.BlockSpec(memory_space=pltpu.SMEM), anyw, anyw, vmem] + [anyw] * (2 * len(mine)),
        out_specs=(vmem, vmem),
        scratch_shapes=buffers + [pltpu.SemaphoreType.DMA((copies,))],
        compiler_params=pltpu.CompilerParams(vmem_limit_bytes=56 << 20),
        name="pruned_ffn",
    )(place, normed, cot, gain, *mine, *theirs)


def final_kernel(place, act, gain, parts, grad):
    share, width = act.shape
    x = act[...].astype(F32)
    inv = lax.rsqrt(jnp.mean(x * x, axis=-1, keepdims=True) + 1e-05)
    dnormed = []
    for j in range(width // BLOCK):
        total = parts[0, j * share : (j + 1) * share, :].astype(F32)
        for src in range(1, SHARDS):
            total += parts[src, j * share : (j + 1) * share, :].astype(F32)
        dnormed.append(total)
    scaled = jnp.concatenate(dnormed, axis=1) * gain[...].astype(F32)
    normalized = x * inv
    mean = jnp.mean(scaled * normalized, axis=-1, keepdims=True)
    grad[...] = (inv * (scaled - normalized * mean)).astype(BF)


def final(place, act, gain, parts):
    tokens, width = act.shape
    share = tokens // SHARDS
    return pl.pallas_call(
        final_kernel,
        out_shape=jax.ShapeDtypeStruct((share, width), BF),
        grid_spec=pltpu.PrefetchScalarGridSpec(
            num_scalar_prefetch=1,
            grid=(1,),
            in_specs=[
                pl.BlockSpec((share, width), lambda i, p: (p[0], 0)),
                pl.BlockSpec((1, width), lambda i, p: (0, 0)),
                pl.BlockSpec(parts.shape, lambda i, p: (0, 0, 0)),
            ],
            out_specs=pl.BlockSpec((share, width), lambda i, p: (0, 0)),
        ),
        compiler_params=pltpu.CompilerParams(vmem_limit_bytes=12 << 20),
        name="input_grad",
    )(place, act, gain.reshape(1, -1), parts)


def whole(x, yh0):
    length = x.shape[0] // BLOCK
    return lax.all_gather(x, "z", axis=0, tiled=True), tuple(((i,), yh0, length) for i in range(Z))


def swapped(x, axis, size, distance):
    return lax.ppermute(x, axis, [(i, i ^ distance) for i in range(size)])


def summed(x, *axes):
    for axis, size in axes:
        distance = 1
        while distance < size:
            x = x + swapped(x, axis, size, distance)
            distance *= 2
    return x


def along_y(x):
    shifted = [lax.ppermute(x, "yh", [(i, (i + k) % YH) for i in range(YH)]) for k in range(1, YH)]
    return jnp.concatenate([x] + shifted, axis=0)


def per_device(
    activations, norm_gain, gate_w, up_w, down_w, mask_gain, kept_blocks, kept_counts, cotangent
):
    me = lax.axis_index(TENSOR)
    place = jnp.stack([me, lax.axis_index("z"), lax.axis_index("core"), lax.axis_index("yh")]).astype(jnp.int32)

    sent = pack(place, kept_blocks, kept_counts, gate_w, up_w, down_w, mask_gain)
    got = lax.all_to_all(sent, TENSOR, split_axis=0, concat_axis=0, tiled=True)
    ends = jnp.cumsum(kept_counts)
    source = jnp.sum((ends <= me).astype(jnp.int32))
    slot = lax.dynamic_index_in_dim(got, source, 0, keepdims=False)
    column = along_y(slot[:BLOCK])
    halves = [whole(part, i * YH // PARTS) for i, part in enumerate(jnp.split(column, PARTS))]
    weights, order = [one for one, _ in halves], tuple(one for _, one in halves)

    cotangent, activations_late, slot, _ = lax.optimization_barrier((cotangent, activations, slot, column))
    unit_gain = slot[BLOCK:, :BLOCK]
    wide = jnp.broadcast_to(cotangent[None], (SHARDS,) + cotangent.shape)
    cot = lax.all_to_all(wide, TENSOR, split_axis=0, concat_axis=0, tiled=True).reshape(-1, cotangent.shape[1])
    act = activations_late.astype(F32)
    inv_rms = lax.rsqrt(jnp.mean(act * act, axis=-1, keepdims=True) + 1e-05)
    normed = (act * inv_rms * norm_gain.astype(F32)).astype(BF)

    other = [lax.ppermute(one, "core", [(0, 1), (1, 0)]) for one in weights]
    parts, unit = ffn(place, normed, cot, unit_gain, order, weights, other)
    got = lax.all_to_all(parts, TENSOR, split_axis=0, concat_axis=0, tiled=True)
    unit = summed(unit, ("core", CORE), ("z", Z))
    unit, got = lax.optimization_barrier((unit, got))
    copies = jnp.broadcast_to(unit[None, :1], (YH * SHARDS, 1, BLOCK))
    units = lax.all_to_all(copies, ("yh",) + TENSOR, split_axis=0, concat_axis=0, tiled=True)
    input_grad = final(place, activations, norm_gain, got)
    width = BLOCK // (Z * YH * CORE)
    units = lax.dynamic_slice_in_dim(units.reshape(YH * SHARDS, BLOCK), lax.axis_index(DP) * width, width, 1)
    count, k = kept_counts[me], jnp.arange(2)
    source = jnp.tile(jnp.arange(SHARDS), YH)
    wanted = (source[None] == ends[me] - count + k[:, None]) & (k < count)[:, None]
    gain_grad = jnp.sum(jnp.where(wanted[:, :, None], units[None], 0.0), axis=1)
    return input_grad, gain_grad


def solution(mesh):
    fine = Mesh(mesh.devices.reshape(Z, YH, CORE, YL, X), DP + TENSOR)
    placed = (
        P(DP, None),
        P(),
        P(DP, TENSOR),
        P(DP, TENSOR),
        P(TENSOR, DP),
        P(TENSOR),
        P(),
        P(),
        P(DP + TENSOR, None),
    )
    return jax.shard_map(
        per_device,
        mesh=fine,
        in_specs=placed,
        out_specs=(P(DP + TENSOR, None), P(TENSOR, DP)),
        check_vma=False,
    )
```

```python
import functools
import math

import jax
import jax.numpy as jnp
from jax import lax
from jax.experimental import pallas as pl
from jax.experimental.pallas import tpu as pltpu
from jax.sharding import Mesh
from jax.sharding import PartitionSpec as P

BLOCK = 128
Z, YH, CORE, YL, X = 8, 4, 2, 2, 4
DP = ("z", "yh", "core")
TENSOR = ("yl", "x")
SHARDS = YL * X
BF, F32 = jnp.bfloat16, jnp.float32
EXTRA = 16
UNITS = (8,)
NT = (((1,), (1,)), ((), ()))


def first_slot(counts_ref, shard):
    total = jnp.int32(0)
    for other in range(SHARDS):
        total += jnp.where(other < shard, counts_ref[other], 0)
    return total


def pack_kernel(place, kept, counts, g0, g1, u0, u1, d0, d1, m0, m1, out):
    first = first_slot(counts, place[0])
    slots = []
    for gate, up, down, gain in ((g0, u0, d0, m0), (g1, u1, d1, m1)):
        body = jnp.concatenate([gate[...], up[...], down[...].T], axis=1)
        row = jnp.broadcast_to(gain[0], (EXTRA, BLOCK))
        slots.append((body, jnp.concatenate([row] * 3, axis=1)))
    for dest in range(SHARDS):
        second = dest == first + 1
        out[dest, :BLOCK, :] = jnp.where(second, slots[1][0], slots[0][0])
        out[dest, BLOCK:, :] = jnp.where(second, slots[1][1], slots[0][1])


def pack(place, kept, counts, gate_w, up_w, down_w, mask_gain):
    rows, units = gate_w.shape
    blocks = units // BLOCK

    def pick(k, kept, place):
        return jnp.clip(kept[place[0], k], 0, blocks - 1)

    cols = [
        pl.BlockSpec((rows, BLOCK), lambda i, p, b, n, k=k: (0, pick(k, b, p)))
        for k in (0, 1)
    ]
    down = [
        pl.BlockSpec((BLOCK, rows), lambda i, p, b, n, k=k: (pick(k, b, p), 0))
        for k in (0, 1)
    ]
    gain = [
        pl.BlockSpec((1, 1, BLOCK), lambda i, p, b, n, k=k: (pick(k, b, p), 0, 0))
        for k in (0, 1)
    ]
    gains = mask_gain.reshape(blocks, 1, BLOCK)
    shape = (SHARDS, BLOCK + EXTRA, 3 * BLOCK)
    return pl.pallas_call(
        pack_kernel,
        out_shape=jax.ShapeDtypeStruct(shape, BF),
        grid_spec=pltpu.PrefetchScalarGridSpec(
            num_scalar_prefetch=3,
            grid=(1,),
            in_specs=cols + cols + down + gain,
            out_specs=pl.BlockSpec(shape, lambda i, *_: (0, 0, 0)),
        ),
        name="pack_slots",
    )(place, kept, counts, gate_w, gate_w, up_w, up_w, down_w, down_w, gains, gains)


def ffn_kernel(scale, layout, place, normed, cot, gain, *refs):
    count = len(layout)
    mine, theirs = refs[:count], refs[count : 2 * count]
    out, unit_out = refs[2 * count : 2 * count + 2]
    n_buf, c_buf = refs[2 * count + 2 : 2 * count + 4]
    a_buf, b_buf = refs[2 * count + 4 : 3 * count + 4], refs[3 * count + 4 : 4 * count + 4]
    sems = refs[-1]
    z, core = place[1], place[2]
    copies, work = [], []

    def copy(source, target):
        one = pltpu.make_async_copy(source, target, sems.at[len(copies)])
        one.start()
        copies.append(one)
        return one

    half = normed.shape[1] // 2
    acts = []
    for source, target in ((normed, n_buf), (cot, c_buf)):
        for k in range(2):
            cols = pl.ds(k * half, half)
            acts.append(copy(source.at[:, cols], target.at[:, cols]))
    for i, pieces in enumerate(layout):
        row = 0
        for shift, yh0, length in pieces:
            rows = pl.ds(row, length * BLOCK)
            both = [
                copy(mine[i].at[rows, :], a_buf[i].at[rows, :]),
                copy(theirs[i].at[rows, :], b_buf[i].at[rows, :]),
            ]
            zz = shift[0] if isinstance(shift, tuple) else lax.rem(z + shift + Z, Z)
            for k in range(length):
                at = (zz * YH + yh0 + k) * (CORE * BLOCK)
                near = pl.multiple_of(at + core * BLOCK, BLOCK)
                other = pl.multiple_of(at + (1 - core) * BLOCK, BLOCK)
                work.append((both if k == 0 else [], near, other, a_buf[i], b_buf[i], row))
                row += BLOCK
    for one in acts:
        one.wait()
    tokens = normed.shape[0]
    gate_up = jnp.zeros((tokens, 2 * BLOCK), F32)
    hidden = jnp.zeros((tokens, BLOCK), F32)
    for waits, near, other, a, b, row in work:
        for one in waits:
            one.wait()
        n2 = jnp.concatenate([n_buf[:, pl.ds(near, BLOCK)], n_buf[:, pl.ds(other, BLOCK)]], axis=1)
        c2 = jnp.concatenate([c_buf[:, pl.ds(near, BLOCK)], c_buf[:, pl.ds(other, BLOCK)]], axis=1)
        w2 = jnp.concatenate([a[row : row + BLOCK, :], b[row : row + BLOCK, :]], axis=0)
        gate_up += jnp.dot(n2, w2[:, : 2 * BLOCK], preferred_element_type=F32)
        hidden += jnp.dot(c2, w2[:, 2 * BLOCK :], preferred_element_type=F32)
    gate, up = gate_up[:, :BLOCK], gate_up[:, BLOCK:]
    sig = jax.nn.sigmoid(gate)
    unit = jnp.sum(gate * sig * up * hidden, axis=0, keepdims=True) * scale
    unit_out[...] = jnp.broadcast_to(unit, unit_out.shape)
    masked = hidden * gain[0:1, :].astype(F32)
    gate_grad = (masked * up * sig * (1.0 + gate * (1.0 - sig))).astype(BF)
    up_grad = (masked * gate * sig).astype(BF)
    grads = jnp.concatenate([gate_grad, up_grad], axis=1)
    share = tokens // SHARDS
    for _, near, other, a, b, row in work:
        for at, w in ((near, a), (other, b)):
            part = lax.dot_general(grads, w[row : row + BLOCK, : 2 * BLOCK], NT, preferred_element_type=F32)
            first = pl.multiple_of(at // BLOCK * share, share)
            out[:, pl.ds(first, share), :] = part.astype(BF).reshape(SHARDS, share, BLOCK)


def ffn(place, normed, cot, gain, layout, mine, theirs):
    tokens, width = normed.shape
    rows = width // BLOCK * (tokens // SHARDS)
    vmem = pl.BlockSpec(memory_space=pltpu.VMEM)
    anyw = pl.BlockSpec(memory_space=pl.ANY)
    scale = 1.0 / math.sqrt(tokens * Z * YH * CORE)
    buffers = [pltpu.VMEM(x.shape, BF) for x in (normed, cot, *mine, *theirs)]
    copies = 4 + 2 * sum(len(pieces) for pieces in layout)
    return pl.pallas_call(
        functools.partial(ffn_kernel, scale, layout),
        out_shape=(
            jax.ShapeDtypeStruct((SHARDS, rows, BLOCK), BF),
            jax.ShapeDtypeStruct(UNITS + (BLOCK,), F32),
        ),
        in_specs=[pl.BlockSpec(memory_space=pltpu.SMEM), anyw, anyw, vmem] + [anyw] * (2 * len(mine)),
        out_specs=(vmem, vmem),
        scratch_shapes=buffers + [pltpu.SemaphoreType.DMA((copies,))],
        compiler_params=pltpu.CompilerParams(vmem_limit_bytes=56 << 20),
        name="pruned_ffn",
    )(place, normed, cot, gain, *mine, *theirs)


def final_kernel(place, act, gain, parts, grad):
    share, width = act.shape
    x = act[...].astype(F32)
    inv = lax.rsqrt(jnp.mean(x * x, axis=-1, keepdims=True) + 1e-05)
    dnormed = []
    for j in range(width // BLOCK):
        total = parts[0, j * share : (j + 1) * share, :].astype(F32)
        for src in range(1, SHARDS):
            total += parts[src, j * share : (j + 1) * share, :].astype(F32)
        dnormed.append(total)
    scaled = jnp.concatenate(dnormed, axis=1) * gain[...].astype(F32)
    normalized = x * inv
    mean = jnp.mean(scaled * normalized, axis=-1, keepdims=True)
    grad[...] = (inv * (scaled - normalized * mean)).astype(BF)


def final(place, act, gain, parts):
    tokens, width = act.shape
    share = tokens // SHARDS
    return pl.pallas_call(
        final_kernel,
        out_shape=jax.ShapeDtypeStruct((share, width), BF),
        grid_spec=pltpu.PrefetchScalarGridSpec(
            num_scalar_prefetch=1,
            grid=(1,),
            in_specs=[
                pl.BlockSpec((share, width), lambda i, p: (p[0], 0)),
                pl.BlockSpec((1, width), lambda i, p: (0, 0)),
                pl.BlockSpec(parts.shape, lambda i, p: (0, 0, 0)),
            ],
            out_specs=pl.BlockSpec((share, width), lambda i, p: (0, 0)),
        ),
        compiler_params=pltpu.CompilerParams(vmem_limit_bytes=12 << 20),
        name="input_grad",
    )(place, act, gain.reshape(1, -1), parts)


def whole(x, yh0):
    length = x.shape[0] // BLOCK
    return lax.all_gather(x, "z", axis=0, tiled=True), tuple(((i,), yh0, length) for i in range(Z))


def swapped(x, axis, size, distance):
    return lax.ppermute(x, axis, [(i, i ^ distance) for i in range(size)])


def summed(x, *axes):
    for axis, size in axes:
        distance = 1
        while distance < size:
            x = x + swapped(x, axis, size, distance)
            distance *= 2
    return x


def per_device(
    activations, norm_gain, gate_w, up_w, down_w, mask_gain, kept_blocks, kept_counts, cotangent
):
    me = lax.axis_index(TENSOR)
    place = jnp.stack([me, lax.axis_index("z"), lax.axis_index("core")]).astype(jnp.int32)

    sent = pack(place, kept_blocks, kept_counts, gate_w, up_w, down_w, mask_gain)
    got = lax.all_to_all(sent, TENSOR, split_axis=0, concat_axis=0, tiled=True)
    ends = jnp.cumsum(kept_counts)
    source = jnp.sum((ends <= me).astype(jnp.int32))
    slot = lax.dynamic_index_in_dim(got, source, 0, keepdims=False)
    column = lax.all_gather(slot[:BLOCK], "yh", axis=0, tiled=True)
    gathered, order = whole(column, 0)
    weights, order = [gathered], (order,)

    cotangent, activations_late, slot, _ = lax.optimization_barrier((cotangent, activations, slot, column))
    unit_gain = slot[BLOCK:, :BLOCK]
    wide = jnp.broadcast_to(cotangent[None], (SHARDS,) + cotangent.shape)
    cot = lax.all_to_all(wide, TENSOR, split_axis=0, concat_axis=0, tiled=True).reshape(-1, cotangent.shape[1])
    act = activations_late.astype(F32)
    inv_rms = lax.rsqrt(jnp.mean(act * act, axis=-1, keepdims=True) + 1e-05)
    normed = (act * inv_rms * norm_gain.astype(F32)).astype(BF)

    other = [lax.ppermute(one, "core", [(0, 1), (1, 0)]) for one in weights]
    parts, unit = ffn(place, normed, cot, unit_gain, order, weights, other)
    got = lax.all_to_all(parts, TENSOR, split_axis=0, concat_axis=0, tiled=True)
    unit = summed(unit, ("core", CORE), ("z", Z))
    unit, got = lax.optimization_barrier((unit, got))
    copies = jnp.broadcast_to(unit[None, :1], (YH * SHARDS, 1, BLOCK))
    units = lax.all_to_all(copies, ("yh",) + TENSOR, split_axis=0, concat_axis=0, tiled=True)
    input_grad = final(place, activations, norm_gain, got)
    width = BLOCK // (Z * YH * CORE)
    units = lax.dynamic_slice_in_dim(units.reshape(YH * SHARDS, BLOCK), lax.axis_index(DP) * width, width, 1)
    count, k = kept_counts[me], jnp.arange(2)
    source = jnp.tile(jnp.arange(SHARDS), YH)
    wanted = (source[None] == ends[me] - count + k[:, None]) & (k < count)[:, None]
    gain_grad = jnp.sum(jnp.where(wanted[:, :, None], units[None], 0.0), axis=1)
    return input_grad, gain_grad


def solution(mesh):
    fine = Mesh(mesh.devices.reshape(Z, YH, CORE, YL, X), DP + TENSOR)
    placed = (
        P(DP, None),
        P(),
        P(DP, TENSOR),
        P(DP, TENSOR),
        P(TENSOR, DP),
        P(TENSOR),
        P(),
        P(),
        P(DP + TENSOR, None),
    )
    return jax.shard_map(
        per_device,
        mesh=fine,
        in_specs=placed,
        out_specs=(P(DP + TENSOR, None), P(TENSOR, DP)),
        check_vma=False,
    )
```

```python
import functools
import math

import jax
import jax.numpy as jnp
from jax import lax
from jax.experimental import pallas as pl
from jax.experimental.pallas import tpu as pltpu
from jax.sharding import Mesh
from jax.sharding import PartitionSpec as P

BLOCK = 128
Z, YH, CORE, YL, X = 8, 4, 2, 2, 4
DP = ("z", "yh", "core")
TENSOR = ("yl", "x")
SHARDS = YL * X
BF, F32 = jnp.bfloat16, jnp.float32
NT = (((1,), (1,)), ((), ()))


def pack_kernel(me, kept, counts, g0, g1, u0, u1, d0, d1, out):
    first = jnp.int32(0)
    for shard in range(SHARDS):
        first += jnp.where(shard < me[0], counts[shard], 0)
    slots = [
        jnp.concatenate([gate[...], up[...], down[...].T], axis=1)
        for gate, up, down in ((g0, u0, d0), (g1, u1, d1))
    ]
    for dest in range(SHARDS):
        out[dest] = jnp.where(dest == first + 1, slots[1], slots[0])


def pack(me, kept, counts, gate_w, up_w, down_w):
    rows, units = gate_w.shape

    def block(kept, me, k):
        return jnp.clip(kept[me[0], k], 0, units // BLOCK - 1)

    cols = [pl.BlockSpec((rows, BLOCK), lambda i, m, b, n, k=k: (0, block(b, m, k))) for k in (0, 1)]
    down = [pl.BlockSpec((BLOCK, rows), lambda i, m, b, n, k=k: (block(b, m, k), 0)) for k in (0, 1)]
    shape = (SHARDS, BLOCK, 3 * BLOCK)
    return pl.pallas_call(
        pack_kernel,
        out_shape=jax.ShapeDtypeStruct(shape, BF),
        grid_spec=pltpu.PrefetchScalarGridSpec(
            num_scalar_prefetch=3,
            grid=(1,),
            in_specs=cols + cols + down,
            out_specs=pl.BlockSpec(shape, lambda i, *_: (0, 0, 0)),
        ),
        name="pack_slots",
    )(me, kept, counts, gate_w, gate_w, up_w, up_w, down_w, down_w)


def ffn_kernel(scale, normed, cot, gain, weights, out, unit_out, n_buf, c_buf, w_buf, sems):
    chunk = normed.shape[1] // Z
    copies = []
    for i in range(Z):
        part = pl.ds(i * chunk, chunk)
        views = ((normed, n_buf, (slice(None), part)), (cot, c_buf, (slice(None), part)), (weights, w_buf, (part, slice(None))))
        for j, (source, target, at) in enumerate(views):
            one = pltpu.make_async_copy(source.at[at], target.at[at], sems.at[3 * i + j])
            one.start()
            copies.append(one)
    tokens = normed.shape[0]
    gate_up = jnp.zeros((tokens, 2 * BLOCK), F32)
    hidden = jnp.zeros((tokens, BLOCK), F32)
    rows = [
        [((z * CORE + core) * YH + yh) * BLOCK for core in range(CORE)]
        for z in range(Z) for yh in range(YH)
    ]
    wide = CORE * BLOCK
    for i, pair in enumerate(rows):
        if i % YH == 0:
            for one in copies[3 * (i // YH) : 3 * (i // YH) + 3]:
                one.wait()
        w2 = jnp.concatenate([w_buf[row : row + BLOCK, :] for row in pair], axis=0)
        gate_up += jnp.dot(n_buf[:, i * wide : (i + 1) * wide], w2[:, : 2 * BLOCK], preferred_element_type=F32)
        hidden += jnp.dot(c_buf[:, i * wide : (i + 1) * wide], w2[:, 2 * BLOCK :], preferred_element_type=F32)
    gate, up = gate_up[:, :BLOCK], gate_up[:, BLOCK:]
    sig = jax.nn.sigmoid(gate)
    unit = jnp.sum(gate * sig * up * hidden, axis=0, keepdims=True) * scale
    unit_out[...] = jnp.broadcast_to(unit, unit_out.shape)
    masked = hidden * gain[0:1, :].astype(F32)
    gate_grad = (masked * up * sig * (1.0 + gate * (1.0 - sig))).astype(BF)
    up_grad = (masked * gate * sig).astype(BF)
    grads = jnp.concatenate([gate_grad, up_grad], axis=1)
    share = tokens // SHARDS
    for i, pair in enumerate(rows):
        w2 = jnp.concatenate([w_buf[row : row + BLOCK, : 2 * BLOCK] for row in pair], axis=0)
        part = lax.dot_general(grads, w2, NT, preferred_element_type=F32).astype(BF)
        for core in range(CORE):
            block = part[:, core * BLOCK : (core + 1) * BLOCK].reshape(SHARDS, share, BLOCK)
            first = (i * CORE + core) * share
            out[:, first : first + share, :] = block


def ffn(normed, cot, gain, weights):
    tokens, width = normed.shape
    rows = width // BLOCK * (tokens // SHARDS)
    vmem = pl.BlockSpec(memory_space=pltpu.VMEM)
    anyw = pl.BlockSpec(memory_space=pl.ANY)
    scale = 1.0 / math.sqrt(tokens * Z * YH * CORE)
    buffers = [pltpu.VMEM(x.shape, BF) for x in (normed, cot, weights)]
    return pl.pallas_call(
        functools.partial(ffn_kernel, scale),
        out_shape=(
            jax.ShapeDtypeStruct((SHARDS, rows, BLOCK), BF),
            jax.ShapeDtypeStruct((8, BLOCK), F32),
        ),
        in_specs=[anyw, anyw, vmem, anyw],
        out_specs=(vmem, vmem),
        scratch_shapes=buffers + [pltpu.SemaphoreType.DMA((3 * Z,))],
        compiler_params=pltpu.CompilerParams(vmem_limit_bytes=56 << 20),
        name="pruned_ffn",
    )(normed, cot, gain, weights)


def final_kernel(place, act, gain, parts, grad):
    share, width = act.shape
    x = act[...].astype(F32)
    inv = lax.rsqrt(jnp.mean(x * x, axis=-1, keepdims=True) + 1e-05)
    dnormed = []
    for j in range(width // BLOCK):
        total = parts[0, j * share : (j + 1) * share, :].astype(F32)
        for src in range(1, SHARDS):
            total += parts[src, j * share : (j + 1) * share, :].astype(F32)
        dnormed.append(total)
    scaled = jnp.concatenate(dnormed, axis=1) * gain[...].astype(F32)
    normalized = x * inv
    mean = jnp.mean(scaled * normalized, axis=-1, keepdims=True)
    grad[...] = (inv * (scaled - normalized * mean)).astype(BF)


def final(place, act, gain, parts):
    tokens, width = act.shape
    share = tokens // SHARDS
    return pl.pallas_call(
        final_kernel,
        out_shape=jax.ShapeDtypeStruct((share, width), BF),
        grid_spec=pltpu.PrefetchScalarGridSpec(
            num_scalar_prefetch=1,
            grid=(1,),
            in_specs=[
                pl.BlockSpec((share, width), lambda i, p: (p[0], 0)),
                pl.BlockSpec((1, width), lambda i, p: (0, 0)),
                pl.BlockSpec(parts.shape, lambda i, p: (0, 0, 0)),
            ],
            out_specs=pl.BlockSpec((share, width), lambda i, p: (0, 0)),
        ),
        compiler_params=pltpu.CompilerParams(vmem_limit_bytes=12 << 20),
        name="input_grad",
    )(place, act, gain.reshape(1, -1), parts)


def per_device(
    activations, norm_gain, gate_w, up_w, down_w, mask_gain, kept_blocks, kept_counts, cotangent
):
    me = lax.axis_index(TENSOR)
    shards, k = jnp.arange(SHARDS), jnp.arange(2)
    blocks = mask_gain.shape[0] // BLOCK
    sent = pack(me.reshape(1), kept_blocks, kept_counts, gate_w, up_w, down_w)
    got = lax.all_to_all(sent, TENSOR, split_axis=0, concat_axis=0, tiled=True)
    ends = jnp.cumsum(kept_counts)
    source = jnp.minimum(jnp.sum((ends <= me).astype(jnp.int32)), SHARDS - 1)
    slot = lax.dynamic_index_in_dim(got, source, 0, keepdims=False)
    column = lax.all_gather(slot, "yh", axis=0, tiled=True)
    weights = lax.all_gather(column, ("z", "core"), axis=0, tiled=True)

    late, _ = lax.optimization_barrier(((cotangent, activations, mask_gain, kept_blocks, kept_counts), column))
    cotangent, act, mask_gain, kept_blocks, kept_counts = late
    kept = jnp.clip(kept_blocks[me], 0, blocks - 1)
    first = jnp.sum(jnp.where(shards < me, kept_counts, 0))
    copies = jnp.broadcast_to(cotangent[None], (SHARDS,) + cotangent.shape)
    cot = lax.all_to_all(copies, TENSOR, split_axis=0, concat_axis=0, tiled=True)
    cot = cot.reshape(-1, cotangent.shape[1])
    act = act.astype(F32)
    inv_rms = lax.rsqrt(jnp.mean(act * act, axis=-1, keepdims=True) + 1e-05)
    normed = (act * inv_rms * norm_gain.astype(F32)).astype(BF)
    gains = jnp.take(mask_gain.reshape(blocks, BLOCK), kept, axis=0)
    gains = lax.all_gather(gains, TENSOR, axis=0, tiled=True)
    which = me - jnp.sum(jnp.where(shards == source, ends - kept_counts, 0))
    unit_gain = lax.dynamic_slice_in_dim(gains, source * 2 + jnp.clip(which, 0, 1), 1, 0)

    parts, unit = ffn(normed, cot, unit_gain, weights)
    got = lax.all_to_all(parts, TENSOR, split_axis=0, concat_axis=0, tiled=True)
    unit = unit + lax.ppermute(unit, "core", [(0, 1), (1, 0)])
    unit = jnp.sum(lax.all_gather(unit[:1], "z", axis=0, tiled=True), axis=0)
    unit, got = lax.optimization_barrier((unit, got))
    copies = jnp.broadcast_to(unit[None, None], (YH * SHARDS, 1, BLOCK))
    units = lax.all_to_all(copies, ("yh",) + TENSOR, split_axis=0, concat_axis=0, tiled=True)
    input_grad = final(me.reshape(1), activations, norm_gain, got)
    width = BLOCK // (Z * YH * CORE)
    units = lax.dynamic_slice_in_dim(units.reshape(YH * SHARDS, BLOCK), lax.axis_index(DP) * width, width, 1)
    count = kept_counts[me]
    owner = jnp.tile(shards, YH)
    wanted = (owner[None] == first + k[:, None]) & (k < count)[:, None]
    gain_grad = jnp.sum(jnp.where(wanted[:, :, None], units[None], 0.0), axis=1)
    return input_grad, gain_grad


def solution(mesh):
    fine = Mesh(mesh.devices.reshape(Z, YH, CORE, YL, X), DP + TENSOR)
    placed = (
        P(DP, None),
        P(),
        P(DP, TENSOR),
        P(DP, TENSOR),
        P(TENSOR, DP),
        P(TENSOR),
        P(),
        P(),
        P(DP + TENSOR, None),
    )
    return jax.shard_map(
        per_device,
        mesh=fine,
        in_specs=placed,
        out_specs=(P(DP + TENSOR, None), P(TENSOR, DP)),
        check_vma=False,
    )
```

```python
import functools
import math

import jax
import jax.numpy as jnp
from jax import lax
from jax.experimental import pallas as pl
from jax.experimental.pallas import tpu as pltpu
from jax.sharding import Mesh
from jax.sharding import PartitionSpec as P

BLOCK = 128
Z, YH, CORE, YL, X = 8, 4, 2, 2, 4
DP = ("z", "yh", "core")
TENSOR = ("yl", "x")
SHARDS = YL * X
BF, F32 = jnp.bfloat16, jnp.float32
EXTRA = 16
NT = (((1,), (1,)), ((), ()))


def pack_kernel(me, kept, counts, g0, g1, u0, u1, d0, d1, m0, m1, out):
    first = jnp.int32(0)
    for shard in range(SHARDS):
        first += jnp.where(shard < me[0], counts[shard], 0)
    slots = []
    for gate, up, down, gain in ((g0, u0, d0, m0), (g1, u1, d1, m1)):
        body = jnp.concatenate([gate[...], up[...], down[...].T], axis=1)
        row = jnp.broadcast_to(gain[0], (EXTRA, BLOCK))
        slots.append((body, jnp.concatenate([row] * 3, axis=1)))
    for dest in range(SHARDS):
        second = dest == first + 1
        out[dest, :BLOCK, :] = jnp.where(second, slots[1][0], slots[0][0])
        out[dest, BLOCK:, :] = jnp.where(second, slots[1][1], slots[0][1])


def pack(me, kept, counts, gate_w, up_w, down_w, mask_gain):
    rows, units = gate_w.shape

    def block(kept, me, k):
        return jnp.clip(kept[me[0], k], 0, units // BLOCK - 1)

    cols = [pl.BlockSpec((rows, BLOCK), lambda i, m, b, n, k=k: (0, block(b, m, k))) for k in (0, 1)]
    down = [pl.BlockSpec((BLOCK, rows), lambda i, m, b, n, k=k: (block(b, m, k), 0)) for k in (0, 1)]
    gain = [pl.BlockSpec((1, 1, BLOCK), lambda i, m, b, n, k=k: (block(b, m, k), 0, 0)) for k in (0, 1)]
    gains = mask_gain.reshape(units // BLOCK, 1, BLOCK)
    shape = (SHARDS, BLOCK + EXTRA, 3 * BLOCK)
    return pl.pallas_call(
        pack_kernel,
        out_shape=jax.ShapeDtypeStruct(shape, BF),
        grid_spec=pltpu.PrefetchScalarGridSpec(
            num_scalar_prefetch=3,
            grid=(1,),
            in_specs=cols + cols + down + gain,
            out_specs=pl.BlockSpec(shape, lambda i, *_: (0, 0, 0)),
        ),
        name="pack_slots",
    )(me, kept, counts, gate_w, gate_w, up_w, up_w, down_w, down_w, gains, gains)


def ffn_kernel(scale, layout, place, normed, cot, gain, *refs):
    count = len(layout)
    mine, theirs = refs[:count], refs[count : 2 * count]
    out, unit_out = refs[2 * count : 2 * count + 2]
    n_buf, c_buf = refs[2 * count + 2 : 2 * count + 4]
    a_buf, b_buf = refs[2 * count + 4 : 3 * count + 4], refs[3 * count + 4 : 4 * count + 4]
    sems = refs[-1]
    z, core = place[0], place[1]
    copies, work = [], []

    def copy(source, target):
        one = pltpu.make_async_copy(source, target, sems.at[len(copies)])
        one.start()
        copies.append(one)
        return one

    half = normed.shape[1] // 2
    acts = []
    for source, target in ((normed, n_buf), (cot, c_buf)):
        for k in range(2):
            cols = pl.ds(k * half, half)
            acts.append(copy(source.at[:, cols], target.at[:, cols]))
    for i, pieces in enumerate(layout):
        row = 0
        for shift, yh0, length in pieces:
            rows = pl.ds(row, length * BLOCK)
            both = [
                copy(mine[i].at[rows, :], a_buf[i].at[rows, :]),
                copy(theirs[i].at[rows, :], b_buf[i].at[rows, :]),
            ]
            zz = lax.rem(z + shift + Z, Z)
            for k in range(length):
                at = (zz * YH + yh0 + k) * (CORE * BLOCK)
                near = pl.multiple_of(at + core * BLOCK, BLOCK)
                other = pl.multiple_of(at + (1 - core) * BLOCK, BLOCK)
                work.append((both if k == 0 else [], near, other, a_buf[i], b_buf[i], row))
                row += BLOCK
    for one in acts:
        one.wait()
    tokens = normed.shape[0]
    gate_up = jnp.zeros((tokens, 2 * BLOCK), F32)
    hidden = jnp.zeros((tokens, BLOCK), F32)
    for waits, near, other, a, b, row in work:
        for one in waits:
            one.wait()
        n2 = jnp.concatenate([n_buf[:, pl.ds(near, BLOCK)], n_buf[:, pl.ds(other, BLOCK)]], axis=1)
        c2 = jnp.concatenate([c_buf[:, pl.ds(near, BLOCK)], c_buf[:, pl.ds(other, BLOCK)]], axis=1)
        w2 = jnp.concatenate([a[row : row + BLOCK, :], b[row : row + BLOCK, :]], axis=0)
        gate_up += jnp.dot(n2, w2[:, : 2 * BLOCK], preferred_element_type=F32)
        hidden += jnp.dot(c2, w2[:, 2 * BLOCK :], preferred_element_type=F32)
    gate, up = gate_up[:, :BLOCK], gate_up[:, BLOCK:]
    sig = jax.nn.sigmoid(gate)
    unit = jnp.sum(gate * sig * up * hidden, axis=0, keepdims=True) * scale
    unit_out[...] = jnp.broadcast_to(unit, unit_out.shape)
    masked = hidden * gain[0:1, :].astype(F32)
    gate_grad = (masked * up * sig * (1.0 + gate * (1.0 - sig))).astype(BF)
    up_grad = (masked * gate * sig).astype(BF)
    grads = jnp.concatenate([gate_grad, up_grad], axis=1)
    share = tokens // SHARDS
    for _, near, other, a, b, row in work:
        for at, w in ((near, a), (other, b)):
            part = lax.dot_general(grads, w[row : row + BLOCK, : 2 * BLOCK], NT, preferred_element_type=F32)
            first = pl.multiple_of(at // BLOCK * share, share)
            out[:, pl.ds(first, share), :] = part.astype(BF).reshape(SHARDS, share, BLOCK)


def ffn(place, normed, cot, gain, layout, mine, theirs):
    tokens, width = normed.shape
    rows = width // BLOCK * (tokens // SHARDS)
    vmem = pl.BlockSpec(memory_space=pltpu.VMEM)
    anyw = pl.BlockSpec(memory_space=pl.ANY)
    scale = 1.0 / math.sqrt(tokens * Z * YH * CORE)
    buffers = [pltpu.VMEM(x.shape, BF) for x in (normed, cot, *mine, *theirs)]
    copies = 4 + 2 * sum(len(pieces) for pieces in layout)
    return pl.pallas_call(
        functools.partial(ffn_kernel, scale, layout),
        out_shape=(
            jax.ShapeDtypeStruct((SHARDS, rows, BLOCK), BF),
            jax.ShapeDtypeStruct((8, BLOCK), F32),
        ),
        in_specs=[pl.BlockSpec(memory_space=pltpu.SMEM), anyw, anyw, vmem] + [anyw] * (2 * len(mine)),
        out_specs=(vmem, vmem),
        scratch_shapes=buffers + [pltpu.SemaphoreType.DMA((copies,))],
        compiler_params=pltpu.CompilerParams(vmem_limit_bytes=56 << 20),
        name="pruned_ffn",
    )(place, normed, cot, gain, *mine, *theirs)


def final_kernel(place, act, gain, parts, grad):
    share, width = act.shape
    x = act[...].astype(F32)
    inv = lax.rsqrt(jnp.mean(x * x, axis=-1, keepdims=True) + 1e-05)
    dnormed = []
    for j in range(width // BLOCK):
        total = parts[0, j * share : (j + 1) * share, :].astype(F32)
        for src in range(1, SHARDS):
            total += parts[src, j * share : (j + 1) * share, :].astype(F32)
        dnormed.append(total)
    scaled = jnp.concatenate(dnormed, axis=1) * gain[...].astype(F32)
    normalized = x * inv
    mean = jnp.mean(scaled * normalized, axis=-1, keepdims=True)
    grad[...] = (inv * (scaled - normalized * mean)).astype(BF)


def final(place, act, gain, parts):
    tokens, width = act.shape
    share = tokens // SHARDS
    return pl.pallas_call(
        final_kernel,
        out_shape=jax.ShapeDtypeStruct((share, width), BF),
        grid_spec=pltpu.PrefetchScalarGridSpec(
            num_scalar_prefetch=1,
            grid=(1,),
            in_specs=[
                pl.BlockSpec((share, width), lambda i, p: (p[0], 0)),
                pl.BlockSpec((1, width), lambda i, p: (0, 0)),
                pl.BlockSpec(parts.shape, lambda i, p: (0, 0, 0)),
            ],
            out_specs=pl.BlockSpec((share, width), lambda i, p: (0, 0)),
        ),
        compiler_params=pltpu.CompilerParams(vmem_limit_bytes=12 << 20),
        name="input_grad",
    )(place, act, gain.reshape(1, -1), parts)


def ring(x):
    up = [(i, (i + 1) % Z) for i in range(Z)]
    down = [(i, (i - 1) % Z) for i in range(Z)]
    chunks, order, a, b = [x], [(0, 0, YH)], x, x
    for step in (1, 2, 3):
        a, b = lax.ppermute(a, "z", up), lax.ppermute(b, "z", down)
        chunks += [a, b]
        order += [(-step, 0, YH), (step, 0, YH)]
    half = x.shape[0] // 2
    far = [lax.ppermute(a[:half], "z", up), lax.ppermute(b[half:], "z", down)]
    arrays = [jnp.concatenate(chunks, axis=0), jnp.concatenate(far, axis=0)]
    return arrays, (tuple(order), ((Z // 2, 0, YH),)), chunks[1]


def per_device(
    activations, norm_gain, gate_w, up_w, down_w, mask_gain, kept_blocks, kept_counts, cotangent
):
    me = lax.axis_index(TENSOR)
    sent = pack(me.reshape(1), kept_blocks, kept_counts, gate_w, up_w, down_w, mask_gain)
    copies = jnp.broadcast_to(cotangent[None], (SHARDS,) + cotangent.shape)
    got = lax.all_to_all(sent, TENSOR, split_axis=0, concat_axis=0, tiled=True)
    ends = jnp.cumsum(kept_counts)
    source = jnp.minimum(jnp.sum((ends <= me).astype(jnp.int32)), SHARDS - 1)
    slot = lax.dynamic_index_in_dim(got, source, 0, keepdims=False)
    column = lax.all_gather(slot[:BLOCK], "yh", axis=0, tiled=True)
    weights, layout, early = ring(column)
    others = [lax.ppermute(one, "core", [(0, 1), (1, 0)]) for one in weights]

    late, _ = lax.optimization_barrier(((copies, activations, slot), early))
    copies, act, slot = late
    cot = lax.all_to_all(copies, TENSOR, split_axis=0, concat_axis=0, tiled=True)
    cot = cot.reshape(-1, cotangent.shape[1])
    act = act.astype(F32)
    inv_rms = lax.rsqrt(jnp.mean(act * act, axis=-1, keepdims=True) + 1e-05)
    normed = (act * inv_rms * norm_gain.astype(F32)).astype(BF)
    place = jnp.stack([lax.axis_index("z"), lax.axis_index("core")]).astype(jnp.int32)

    parts, unit = ffn(place, normed, cot, slot[BLOCK:, :BLOCK], layout, weights, others)
    got = lax.all_to_all(parts, TENSOR, split_axis=0, concat_axis=0, tiled=True)
    unit = unit + lax.ppermute(unit, "core", [(0, 1), (1, 0)])
    unit = jnp.sum(lax.all_gather(unit[:1], "z", axis=0, tiled=True), axis=0, keepdims=True)
    unit = jnp.sum(lax.all_gather(unit, "yh", axis=0, tiled=True), axis=0)
    unit, got = lax.optimization_barrier((unit, got))
    wide = jnp.broadcast_to(unit[None, None], (SHARDS, 1, BLOCK))
    units = lax.all_to_all(wide, TENSOR, split_axis=0, concat_axis=0, tiled=True)
    input_grad = final(me.reshape(1), activations, norm_gain, got)
    width = BLOCK // (Z * YH * CORE)
    units = lax.dynamic_slice_in_dim(units.reshape(SHARDS, BLOCK), lax.axis_index(DP) * width, width, 1)
    shards, k = jnp.arange(SHARDS), jnp.arange(2)
    count = kept_counts[me]
    wanted = (shards[None] == ends[me] - count + k[:, None]) & (k < count)[:, None]
    gain_grad = jnp.sum(jnp.where(wanted[:, :, None], units[None], 0.0), axis=1)
    return input_grad, gain_grad


def solution(mesh):
    fine = Mesh(mesh.devices.reshape(Z, YH, CORE, YL, X), DP + TENSOR)
    placed = (
        P(DP, None),
        P(),
        P(DP, TENSOR),
        P(DP, TENSOR),
        P(TENSOR, DP),
        P(TENSOR),
        P(),
        P(),
        P(DP + TENSOR, None),
    )
    return jax.shard_map(
        per_device,
        mesh=fine,
        in_specs=placed,
        out_specs=(P(DP + TENSOR, None), P(TENSOR, DP)),
        check_vma=False,
    )
```

```python
import functools
import math

import jax
import jax.numpy as jnp
from jax import lax
from jax.experimental import pallas as pl
from jax.experimental.pallas import tpu as pltpu
from jax.sharding import Mesh
from jax.sharding import PartitionSpec as P

BLOCK = 128
Z, YH, CORE, YL, X = 8, 4, 2, 2, 4
DP = ("z", "yh", "core")
TENSOR = ("yl", "x")
SHARDS = YL * X
BF, F32 = jnp.bfloat16, jnp.float32
NT = (((1,), (1,)), ((), ()))


def pack_kernel(me, kept, counts, g0, g1, u0, u1, d0, d1, out):
    first = jnp.int32(0)
    for shard in range(SHARDS):
        first += jnp.where(shard < me[0], counts[shard], 0)
    slots = [
        jnp.concatenate([gate[...], up[...], down[...].T], axis=1)
        for gate, up, down in ((g0, u0, d0), (g1, u1, d1))
    ]
    for dest in range(SHARDS):
        out[dest] = jnp.where(dest == first + 1, slots[1], slots[0])


def pack(me, kept, counts, gate_w, up_w, down_w):
    rows, units = gate_w.shape

    def block(kept, me, k):
        return jnp.clip(kept[me[0], k], 0, units // BLOCK - 1)

    cols = [pl.BlockSpec((rows, BLOCK), lambda i, m, b, n, k=k: (0, block(b, m, k))) for k in (0, 1)]
    down = [pl.BlockSpec((BLOCK, rows), lambda i, m, b, n, k=k: (block(b, m, k), 0)) for k in (0, 1)]
    shape = (SHARDS, BLOCK, 3 * BLOCK)
    return pl.pallas_call(
        pack_kernel,
        out_shape=jax.ShapeDtypeStruct(shape, BF),
        grid_spec=pltpu.PrefetchScalarGridSpec(
            num_scalar_prefetch=3,
            grid=(1,),
            in_specs=cols + cols + down,
            out_specs=pl.BlockSpec(shape, lambda i, *_: (0, 0, 0)),
        ),
        name="pack_slots",
    )(me, kept, counts, gate_w, gate_w, up_w, up_w, down_w, down_w)


def ffn_kernel(scale, normed, cot, gain, weights, out, unit_out, n_buf, c_buf, w_buf, sems):
    chunk = normed.shape[1] // Z
    copies = []
    for i in range(Z):
        part = pl.ds(i * chunk, chunk)
        views = ((normed, n_buf, (slice(None), part)), (cot, c_buf, (slice(None), part)), (weights, w_buf, (part, slice(None))))
        for j, (source, target, at) in enumerate(views):
            one = pltpu.make_async_copy(source.at[at], target.at[at], sems.at[3 * i + j])
            one.start()
            copies.append(one)
    tokens = normed.shape[0]
    gate_up = jnp.zeros((tokens, 2 * BLOCK), F32)
    hidden = jnp.zeros((tokens, BLOCK), F32)
    rows = [
        [((z * CORE + core) * YH + yh) * BLOCK for core in range(CORE)]
        for z in range(Z) for yh in range(YH)
    ]
    wide = CORE * BLOCK
    for i, pair in enumerate(rows):
        if i % YH == 0:
            for one in copies[3 * (i // YH) : 3 * (i // YH) + 3]:
                one.wait()
        w2 = jnp.concatenate([w_buf[row : row + BLOCK, :] for row in pair], axis=0)
        gate_up += jnp.dot(n_buf[:, i * wide : (i + 1) * wide], w2[:, : 2 * BLOCK], preferred_element_type=F32)
        hidden += jnp.dot(c_buf[:, i * wide : (i + 1) * wide], w2[:, 2 * BLOCK :], preferred_element_type=F32)
    gate, up = gate_up[:, :BLOCK], gate_up[:, BLOCK:]
    sig = jax.nn.sigmoid(gate)
    unit = jnp.sum(gate * sig * up * hidden, axis=0, keepdims=True) * scale
    unit_out[...] = jnp.broadcast_to(unit, unit_out.shape)
    masked = hidden * gain[0:1, :].astype(F32)
    gate_grad = (masked * up * sig * (1.0 + gate * (1.0 - sig))).astype(BF)
    up_grad = (masked * gate * sig).astype(BF)
    grads = jnp.concatenate([gate_grad, up_grad], axis=1)
    share = tokens // SHARDS
    for i, pair in enumerate(rows):
        w2 = jnp.concatenate([w_buf[row : row + BLOCK, : 2 * BLOCK] for row in pair], axis=0)
        part = lax.dot_general(grads, w2, NT, preferred_element_type=F32).astype(BF)
        for core in range(CORE):
            block = part[:, core * BLOCK : (core + 1) * BLOCK].reshape(SHARDS, share, BLOCK)
            first = (i * CORE + core) * share
            out[:, first : first + share, :] = block


def ffn(normed, cot, gain, weights):
    tokens, width = normed.shape
    rows = width // BLOCK * (tokens // SHARDS)
    vmem = pl.BlockSpec(memory_space=pltpu.VMEM)
    anyw = pl.BlockSpec(memory_space=pl.ANY)
    scale = 1.0 / math.sqrt(tokens * Z * YH * CORE)
    buffers = [pltpu.VMEM(x.shape, BF) for x in (normed, cot, weights)]
    return pl.pallas_call(
        functools.partial(ffn_kernel, scale),
        out_shape=(
            jax.ShapeDtypeStruct((SHARDS, rows, BLOCK), BF),
            jax.ShapeDtypeStruct((8, BLOCK), F32),
        ),
        in_specs=[anyw, anyw, vmem, anyw],
        out_specs=(vmem, vmem),
        scratch_shapes=buffers + [pltpu.SemaphoreType.DMA((3 * Z,))],
        compiler_params=pltpu.CompilerParams(vmem_limit_bytes=56 << 20),
        name="pruned_ffn",
    )(normed, cot, gain, weights)


def final_kernel(place, act, gain, parts, grad):
    share, width = act.shape
    x = act[...].astype(F32)
    inv = lax.rsqrt(jnp.mean(x * x, axis=-1, keepdims=True) + 1e-05)
    dnormed = []
    for j in range(width // BLOCK):
        total = parts[0, j * share : (j + 1) * share, :].astype(F32)
        for src in range(1, SHARDS):
            total += parts[src, j * share : (j + 1) * share, :].astype(F32)
        dnormed.append(total)
    scaled = jnp.concatenate(dnormed, axis=1) * gain[...].astype(F32)
    normalized = x * inv
    mean = jnp.mean(scaled * normalized, axis=-1, keepdims=True)
    grad[...] = (inv * (scaled - normalized * mean)).astype(BF)


def final(place, act, gain, parts):
    tokens, width = act.shape
    share = tokens // SHARDS
    return pl.pallas_call(
        final_kernel,
        out_shape=jax.ShapeDtypeStruct((share, width), BF),
        grid_spec=pltpu.PrefetchScalarGridSpec(
            num_scalar_prefetch=1,
            grid=(1,),
            in_specs=[
                pl.BlockSpec((share, width), lambda i, p: (p[0], 0)),
                pl.BlockSpec((1, width), lambda i, p: (0, 0)),
                pl.BlockSpec(parts.shape, lambda i, p: (0, 0, 0)),
            ],
            out_specs=pl.BlockSpec((share, width), lambda i, p: (0, 0)),
        ),
        compiler_params=pltpu.CompilerParams(vmem_limit_bytes=12 << 20),
        name="input_grad",
    )(place, act, gain.reshape(1, -1), parts)


def pick_kernel(counts, units, out):
    me = lax.axis_index("yl") * X + lax.axis_index("x")
    dp = (lax.axis_index("z") * YH + lax.axis_index("yh")) * CORE + lax.axis_index("core")
    first, count = jnp.int32(0), jnp.int32(0)
    for shard in range(SHARDS):
        first += jnp.where(shard < me, counts[shard], 0)
        count += jnp.where(shard == me, counts[shard], 0)
    lane = lax.broadcasted_iota(jnp.int32, (1, BLOCK), 1)
    width = out.shape[1]
    for k in range(out.shape[0]):
        total = jnp.zeros((1, BLOCK), F32)
        for source in range(SHARDS):
            wanted = (source == first + k) & (k < count)
            total = jnp.where(wanted, units[source], total)
        for i in range(width):
            value = jnp.where(lane == dp * width + i, total, 0.0)
            out[k : k + 1, i : i + 1] = jnp.sum(value, axis=1, keepdims=True)


def pick(counts, units):
    vmem = pl.BlockSpec(memory_space=pltpu.VMEM)
    return pl.pallas_call(
        pick_kernel,
        out_shape=jax.ShapeDtypeStruct((2, BLOCK // (Z * YH * CORE)), F32),
        in_specs=[pl.BlockSpec(memory_space=pltpu.SMEM), vmem],
        out_specs=vmem,
        name="gain_grad",
    )(counts, units)


def per_device(
    activations, norm_gain, gate_w, up_w, down_w, mask_gain, kept_blocks, kept_counts, cotangent
):
    me = lax.axis_index(TENSOR)
    shards = jnp.arange(SHARDS)
    blocks = mask_gain.shape[0] // BLOCK
    sent = pack(me.reshape(1), kept_blocks, kept_counts, gate_w, up_w, down_w)
    got = lax.all_to_all(sent, TENSOR, split_axis=0, concat_axis=0, tiled=True)
    ends = jnp.cumsum(kept_counts)
    source = jnp.minimum(jnp.sum((ends <= me).astype(jnp.int32)), SHARDS - 1)
    slot = lax.dynamic_index_in_dim(got, source, 0, keepdims=False)
    column = lax.all_gather(slot, "yh", axis=0, tiled=True)
    weights = lax.all_gather(column, ("z", "core"), axis=0, tiled=True)

    late, _ = lax.optimization_barrier(((cotangent, activations, mask_gain, kept_blocks, kept_counts), column))
    cotangent, act, mask_gain, kept_blocks, kept_counts = late
    kept = jnp.clip(kept_blocks[me], 0, blocks - 1)
    copies = jnp.broadcast_to(cotangent[None], (SHARDS,) + cotangent.shape)
    cot = lax.all_to_all(copies, TENSOR, split_axis=0, concat_axis=0, tiled=True)
    cot = cot.reshape(-1, cotangent.shape[1])
    act = act.astype(F32)
    inv_rms = lax.rsqrt(jnp.mean(act * act, axis=-1, keepdims=True) + 1e-05)
    normed = (act * inv_rms * norm_gain.astype(F32)).astype(BF)
    gains = jnp.take(mask_gain.reshape(blocks, BLOCK), kept, axis=0)
    gains = lax.all_gather(gains, TENSOR, axis=0, tiled=True)
    which = me - jnp.sum(jnp.where(shards == source, ends - kept_counts, 0))
    unit_gain = lax.dynamic_slice_in_dim(gains, source * 2 + jnp.clip(which, 0, 1), 1, 0)

    parts, unit = ffn(normed, cot, unit_gain, weights)
    unit = unit + lax.ppermute(unit, "core", [(0, 1), (1, 0)])
    parts, unit = lax.optimization_barrier((parts, unit))
    got = lax.all_to_all(parts, TENSOR, split_axis=0, concat_axis=0, tiled=True)
    unit = jnp.sum(lax.all_gather(unit[:1], "z", axis=0, tiled=True), axis=0, keepdims=True)
    unit = jnp.sum(lax.all_gather(unit, "yh", axis=0, tiled=True), axis=0)
    copies = jnp.broadcast_to(unit[None, None], (SHARDS, 1, BLOCK))
    copies, got = lax.optimization_barrier((copies, got))
    units = lax.all_to_all(copies, TENSOR, split_axis=0, concat_axis=0, tiled=True)
    input_grad = final(me.reshape(1), activations, norm_gain, got)
    gain_grad = pick(kept_counts, units)
    return input_grad, gain_grad


def solution(mesh):
    fine = Mesh(mesh.devices.reshape(Z, YH, CORE, YL, X), DP + TENSOR)
    placed = (
        P(DP, None),
        P(),
        P(DP, TENSOR),
        P(DP, TENSOR),
        P(TENSOR, DP),
        P(TENSOR),
        P(),
        P(),
        P(DP + TENSOR, None),
    )
    return jax.shard_map(
        per_device,
        mesh=fine,
        in_specs=placed,
        out_specs=(P(DP + TENSOR, None), P(TENSOR, DP)),
        check_vma=False,
    )
```

```python
import functools
import math

import jax
import jax.numpy as jnp
from jax import lax
from jax.experimental import pallas as pl
from jax.experimental.pallas import tpu as pltpu
from jax.sharding import Mesh
from jax.sharding import PartitionSpec as P

BLOCK = 128
Z, YH, CORE, YL, X = 8, 4, 2, 2, 4
DP = ("z", "yh", "core")
TENSOR = ("yl", "x")
SHARDS = YL * X
BF, F32 = jnp.bfloat16, jnp.float32
EXTRA = 16
NT = (((1,), (1,)), ((), ()))


def pack_kernel(me, kept, counts, g0, g1, u0, u1, d0, d1, m0, m1, out):
    first = jnp.int32(0)
    for shard in range(SHARDS):
        first += jnp.where(shard < me[0], counts[shard], 0)
    slots = []
    for gate, up, down, gain in ((g0, u0, d0, m0), (g1, u1, d1, m1)):
        body = jnp.concatenate([gate[...], up[...], down[...].T], axis=1)
        row = jnp.broadcast_to(gain[0], (EXTRA, BLOCK))
        slots.append((body, jnp.concatenate([row] * 3, axis=1)))
    for dest in range(SHARDS):
        second = dest == first + 1
        out[dest, :BLOCK, :] = jnp.where(second, slots[1][0], slots[0][0])
        out[dest, BLOCK:, :] = jnp.where(second, slots[1][1], slots[0][1])


def pack(me, kept, counts, gate_w, up_w, down_w, mask_gain):
    rows, units = gate_w.shape

    def block(kept, me, k):
        return jnp.clip(kept[me[0], k], 0, units // BLOCK - 1)

    cols = [pl.BlockSpec((rows, BLOCK), lambda i, m, b, n, k=k: (0, block(b, m, k))) for k in (0, 1)]
    down = [pl.BlockSpec((BLOCK, rows), lambda i, m, b, n, k=k: (block(b, m, k), 0)) for k in (0, 1)]
    gain = [pl.BlockSpec((1, 1, BLOCK), lambda i, m, b, n, k=k: (block(b, m, k), 0, 0)) for k in (0, 1)]
    gains = mask_gain.reshape(units // BLOCK, 1, BLOCK)
    shape = (SHARDS, BLOCK + EXTRA, 3 * BLOCK)
    return pl.pallas_call(
        pack_kernel,
        out_shape=jax.ShapeDtypeStruct(shape, BF),
        grid_spec=pltpu.PrefetchScalarGridSpec(
            num_scalar_prefetch=3,
            grid=(1,),
            in_specs=cols + cols + down + gain,
            out_specs=pl.BlockSpec(shape, lambda i, *_: (0, 0, 0)),
        ),
        name="pack_slots",
    )(me, kept, counts, gate_w, gate_w, up_w, up_w, down_w, down_w, gains, gains)


def ffn_kernel(scale, layout, normed, cot, gain, *refs):
    count = len(layout)
    mine, theirs = refs[:count], refs[count : 2 * count]
    out, unit_out = refs[2 * count : 2 * count + 2]
    n_buf, c_buf = refs[2 * count + 2 : 2 * count + 4]
    a_buf, b_buf = refs[2 * count + 4 : 3 * count + 4], refs[3 * count + 4 : 4 * count + 4]
    sems = refs[-1]
    z, core = lax.axis_index("z"), lax.axis_index("core")
    copies, work = [], []

    def copy(source, target):
        one = pltpu.make_async_copy(source, target, sems.at[len(copies)])
        one.start()
        copies.append(one)
        return one

    half = normed.shape[1] // 2
    acts = []
    for source, target in ((normed, n_buf), (cot, c_buf)):
        for k in range(2):
            cols = pl.ds(k * half, half)
            acts.append(copy(source.at[:, cols], target.at[:, cols]))
    for i, pieces in enumerate(layout):
        row = 0
        for shift, yh0, length in pieces:
            rows = pl.ds(row, length * BLOCK)
            both = [
                copy(mine[i].at[rows, :], a_buf[i].at[rows, :]),
                copy(theirs[i].at[rows, :], b_buf[i].at[rows, :]),
            ]
            zz = lax.rem(z + shift + Z, Z)
            for k in range(length):
                at = (zz * YH + yh0 + k) * (CORE * BLOCK)
                near = pl.multiple_of(at + core * BLOCK, BLOCK)
                other = pl.multiple_of(at + (1 - core) * BLOCK, BLOCK)
                work.append((both if k == 0 else [], near, other, a_buf[i], b_buf[i], row))
                row += BLOCK
    for one in acts:
        one.wait()
    tokens = normed.shape[0]
    gate_up = jnp.zeros((tokens, 2 * BLOCK), F32)
    hidden = jnp.zeros((tokens, BLOCK), F32)
    for waits, near, other, a, b, row in work:
        for one in waits:
            one.wait()
        n2 = jnp.concatenate([n_buf[:, pl.ds(near, BLOCK)], n_buf[:, pl.ds(other, BLOCK)]], axis=1)
        c2 = jnp.concatenate([c_buf[:, pl.ds(near, BLOCK)], c_buf[:, pl.ds(other, BLOCK)]], axis=1)
        w2 = jnp.concatenate([a[row : row + BLOCK, :], b[row : row + BLOCK, :]], axis=0)
        gate_up += jnp.dot(n2, w2[:, : 2 * BLOCK], preferred_element_type=F32)
        hidden += jnp.dot(c2, w2[:, 2 * BLOCK :], preferred_element_type=F32)
    gate, up = gate_up[:, :BLOCK], gate_up[:, BLOCK:]
    sig = jax.nn.sigmoid(gate)
    unit = jnp.sum(gate * sig * up * hidden, axis=0, keepdims=True) * scale
    unit_out[...] = jnp.broadcast_to(unit, unit_out.shape)
    masked = hidden * gain[0:1, :].astype(F32)
    gate_grad = (masked * up * sig * (1.0 + gate * (1.0 - sig))).astype(BF)
    up_grad = (masked * gate * sig).astype(BF)
    grads = jnp.concatenate([gate_grad, up_grad], axis=1)
    share = tokens // SHARDS
    for _, near, other, a, b, row in work:
        for at, w in ((near, a), (other, b)):
            part = lax.dot_general(grads, w[row : row + BLOCK, : 2 * BLOCK], NT, preferred_element_type=F32)
            first = pl.multiple_of(at // BLOCK * share, share)
            out[:, pl.ds(first, share), :] = part.astype(BF).reshape(SHARDS, share, BLOCK)


def ffn(normed, cot, gain, layout, mine, theirs):
    tokens, width = normed.shape
    rows = width // BLOCK * (tokens // SHARDS)
    vmem = pl.BlockSpec(memory_space=pltpu.VMEM)
    anyw = pl.BlockSpec(memory_space=pl.ANY)
    scale = 1.0 / math.sqrt(tokens * Z * YH * CORE)
    buffers = [pltpu.VMEM(x.shape, BF) for x in (normed, cot, *mine, *theirs)]
    copies = 4 + 2 * sum(len(pieces) for pieces in layout)
    return pl.pallas_call(
        functools.partial(ffn_kernel, scale, layout),
        out_shape=(
            jax.ShapeDtypeStruct((SHARDS, rows, BLOCK), BF),
            jax.ShapeDtypeStruct((8, BLOCK), F32),
        ),
        in_specs=[anyw, anyw, vmem] + [anyw] * (2 * len(mine)),
        out_specs=(vmem, vmem),
        scratch_shapes=buffers + [pltpu.SemaphoreType.DMA((copies,))],
        compiler_params=pltpu.CompilerParams(vmem_limit_bytes=56 << 20),
        name="pruned_ffn",
    )(normed, cot, gain, *mine, *theirs)


def final_kernel(place, act, gain, parts, grad):
    share, width = act.shape
    x = act[...].astype(F32)
    inv = lax.rsqrt(jnp.mean(x * x, axis=-1, keepdims=True) + 1e-05)
    dnormed = []
    for j in range(width // BLOCK):
        total = parts[0, j * share : (j + 1) * share, :].astype(F32)
        for src in range(1, SHARDS):
            total += parts[src, j * share : (j + 1) * share, :].astype(F32)
        dnormed.append(total)
    scaled = jnp.concatenate(dnormed, axis=1) * gain[...].astype(F32)
    normalized = x * inv
    mean = jnp.mean(scaled * normalized, axis=-1, keepdims=True)
    grad[...] = (inv * (scaled - normalized * mean)).astype(BF)


def final(place, act, gain, parts):
    tokens, width = act.shape
    share = tokens // SHARDS
    return pl.pallas_call(
        final_kernel,
        out_shape=jax.ShapeDtypeStruct((share, width), BF),
        grid_spec=pltpu.PrefetchScalarGridSpec(
            num_scalar_prefetch=1,
            grid=(1,),
            in_specs=[
                pl.BlockSpec((share, width), lambda i, p: (p[0], 0)),
                pl.BlockSpec((1, width), lambda i, p: (0, 0)),
                pl.BlockSpec(parts.shape, lambda i, p: (0, 0, 0)),
            ],
            out_specs=pl.BlockSpec((share, width), lambda i, p: (0, 0)),
        ),
        compiler_params=pltpu.CompilerParams(vmem_limit_bytes=12 << 20),
        name="input_grad",
    )(place, act, gain.reshape(1, -1), parts)


def pick_kernel(counts, units, out):
    me = lax.axis_index("yl") * X + lax.axis_index("x")
    dp = (lax.axis_index("z") * YH + lax.axis_index("yh")) * CORE + lax.axis_index("core")
    first, count = jnp.int32(0), jnp.int32(0)
    for shard in range(SHARDS):
        first += jnp.where(shard < me, counts[shard], 0)
        count += jnp.where(shard == me, counts[shard], 0)
    lane = lax.broadcasted_iota(jnp.int32, (1, BLOCK), 1)
    width = out.shape[1]
    for k in range(out.shape[0]):
        total = jnp.zeros((1, BLOCK), F32)
        for source in range(SHARDS):
            wanted = (source == first + k) & (k < count)
            total = jnp.where(wanted, units[source], total)
        for i in range(width):
            value = jnp.where(lane == dp * width + i, total, 0.0)
            out[k : k + 1, i : i + 1] = jnp.sum(value, axis=1, keepdims=True)


def pick(counts, units):
    vmem = pl.BlockSpec(memory_space=pltpu.VMEM)
    return pl.pallas_call(
        pick_kernel,
        out_shape=jax.ShapeDtypeStruct((2, BLOCK // (Z * YH * CORE)), F32),
        in_specs=[pl.BlockSpec(memory_space=pltpu.SMEM), vmem],
        out_specs=vmem,
        name="gain_grad",
    )(counts, units)


def ring(x):
    up = [(i, (i + 1) % Z) for i in range(Z)]
    down = [(i, (i - 1) % Z) for i in range(Z)]
    chunks, order, a, b = [x], [(0, 0, YH)], x, x
    for step in (1, 2, 3):
        a, b = lax.ppermute(a, "z", up), lax.ppermute(b, "z", down)
        chunks += [a, b]
        order += [(-step, 0, YH), (step, 0, YH)]
    far = lax.ppermute(a, "z", up)
    return [jnp.concatenate(chunks, axis=0), far], (tuple(order), ((-4, 0, YH),)), chunks[1]


def per_device(
    activations, norm_gain, gate_w, up_w, down_w, mask_gain, kept_blocks, kept_counts, cotangent
):
    me = lax.axis_index(TENSOR)
    sent = pack(me.reshape(1), kept_blocks, kept_counts, gate_w, up_w, down_w, mask_gain)
    copies = jnp.broadcast_to(cotangent[None], (SHARDS,) + cotangent.shape)
    got = lax.all_to_all(sent, TENSOR, split_axis=0, concat_axis=0, tiled=True)
    ends = jnp.cumsum(kept_counts)
    source = jnp.minimum(jnp.sum((ends <= me).astype(jnp.int32)), SHARDS - 1)
    slot = lax.dynamic_index_in_dim(got, source, 0, keepdims=False)
    slot, copies = lax.optimization_barrier((slot, copies))
    column = lax.all_gather(slot[:BLOCK], "yh", axis=0, tiled=True)
    weights, layout, early = ring(column)
    others = [lax.ppermute(one, "core", [(0, 1), (1, 0)]) for one in weights]

    late, _ = lax.optimization_barrier(((copies, activations, slot), early))
    copies, act, slot = late
    cot = lax.all_to_all(copies, TENSOR, split_axis=0, concat_axis=0, tiled=True)
    cot = cot.reshape(-1, cotangent.shape[1])
    act = act.astype(F32)
    inv_rms = lax.rsqrt(jnp.mean(act * act, axis=-1, keepdims=True) + 1e-05)
    normed = (act * inv_rms * norm_gain.astype(F32)).astype(BF)

    parts, unit = ffn(normed, cot, slot[BLOCK:, :BLOCK], layout, weights, others)
    got = lax.all_to_all(parts, TENSOR, split_axis=0, concat_axis=0, tiled=True)
    unit = unit + lax.ppermute(unit, "core", [(0, 1), (1, 0)])
    unit = jnp.sum(lax.all_gather(unit[:1], "z", axis=0, tiled=True), axis=0, keepdims=True)
    unit = jnp.sum(lax.all_gather(unit, "yh", axis=0, tiled=True), axis=0)
    wide = jnp.broadcast_to(unit[None, None], (SHARDS, 1, BLOCK))
    wide, got = lax.optimization_barrier((wide, got))
    units = lax.all_to_all(wide, TENSOR, split_axis=0, concat_axis=0, tiled=True)
    input_grad = final(me.reshape(1), activations, norm_gain, got)
    gain_grad = pick(kept_counts, units)
    return input_grad, gain_grad


def solution(mesh):
    fine = Mesh(mesh.devices.reshape(Z, YH, CORE, YL, X), DP + TENSOR)
    placed = (
        P(DP, None),
        P(),
        P(DP, TENSOR),
        P(DP, TENSOR),
        P(TENSOR, DP),
        P(TENSOR),
        P(),
        P(),
        P(DP + TENSOR, None),
    )
    return jax.shard_map(
        per_device,
        mesh=fine,
        in_specs=placed,
        out_specs=(P(DP + TENSOR, None), P(TENSOR, DP)),
        check_vma=False,
    )
```

```python
import functools
import math

import jax
import jax.numpy as jnp
from jax import lax
from jax.experimental import pallas as pl
from jax.experimental.pallas import tpu as pltpu
from jax.sharding import Mesh
from jax.sharding import PartitionSpec as P

BLOCK = 128
Z, YH, CORE, YL, X = 8, 4, 2, 2, 4
DP = ("z", "yh", "core")
TENSOR = ("yl", "x")
SHARDS = YL * X
BF, F32 = jnp.bfloat16, jnp.float32
NT = (((1,), (1,)), ((), ()))


def pack_kernel(me, kept, counts, g0, g1, u0, u1, d0, d1, out):
    first = jnp.int32(0)
    for shard in range(SHARDS):
        first += jnp.where(shard < me[0], counts[shard], 0)
    slots = [
        jnp.concatenate([gate[...], up[...], down[...].T], axis=1)
        for gate, up, down in ((g0, u0, d0), (g1, u1, d1))
    ]
    for dest in range(SHARDS):
        out[dest] = jnp.where(dest == first + 1, slots[1], slots[0])


def pack(me, kept, counts, gate_w, up_w, down_w):
    rows, units = gate_w.shape

    def block(kept, me, k):
        return jnp.clip(kept[me[0], k], 0, units // BLOCK - 1)

    cols = [pl.BlockSpec((rows, BLOCK), lambda i, m, b, n, k=k: (0, block(b, m, k))) for k in (0, 1)]
    down = [pl.BlockSpec((BLOCK, rows), lambda i, m, b, n, k=k: (block(b, m, k), 0)) for k in (0, 1)]
    shape = (SHARDS, BLOCK, 3 * BLOCK)
    return pl.pallas_call(
        pack_kernel,
        out_shape=jax.ShapeDtypeStruct(shape, BF),
        grid_spec=pltpu.PrefetchScalarGridSpec(
            num_scalar_prefetch=3,
            grid=(1,),
            in_specs=cols + cols + down,
            out_specs=pl.BlockSpec(shape, lambda i, *_: (0, 0, 0)),
        ),
        name="pack_slots",
    )(me, kept, counts, gate_w, gate_w, up_w, up_w, down_w, down_w)


def ffn_kernel(scale, normed, cot, gain, weights, out, unit_out, n_buf, c_buf, w_buf, sems):
    chunk = normed.shape[1] // Z
    copies = []
    for i in range(Z):
        part = pl.ds(i * chunk, chunk)
        views = ((normed, n_buf, (slice(None), part)), (cot, c_buf, (slice(None), part)), (weights, w_buf, (part, slice(None))))
        for j, (source, target, at) in enumerate(views):
            one = pltpu.make_async_copy(source.at[at], target.at[at], sems.at[3 * i + j])
            one.start()
            copies.append(one)
    tokens = normed.shape[0]
    gate_up = jnp.zeros((tokens, 2 * BLOCK), F32)
    hidden = jnp.zeros((tokens, BLOCK), F32)
    rows = [
        [((z * CORE + core) * YH + yh) * BLOCK for core in range(CORE)]
        for z in range(Z) for yh in range(YH)
    ]
    wide = CORE * BLOCK
    for i, pair in enumerate(rows):
        if i % YH == 0:
            for one in copies[3 * (i // YH) : 3 * (i // YH) + 3]:
                one.wait()
        w2 = jnp.concatenate([w_buf[row : row + BLOCK, :] for row in pair], axis=0)
        gate_up += jnp.dot(n_buf[:, i * wide : (i + 1) * wide], w2[:, : 2 * BLOCK], preferred_element_type=F32)
        hidden += jnp.dot(c_buf[:, i * wide : (i + 1) * wide], w2[:, 2 * BLOCK :], preferred_element_type=F32)
    gate, up = gate_up[:, :BLOCK], gate_up[:, BLOCK:]
    sig = jax.nn.sigmoid(gate)
    unit = jnp.sum(gate * sig * up * hidden, axis=0, keepdims=True) * scale
    unit_out[...] = jnp.broadcast_to(unit, unit_out.shape)
    masked = hidden * gain[0:1, :].astype(F32)
    gate_grad = (masked * up * sig * (1.0 + gate * (1.0 - sig))).astype(BF)
    up_grad = (masked * gate * sig).astype(BF)
    grads = jnp.concatenate([gate_grad, up_grad], axis=1)
    share = tokens // SHARDS
    for i, pair in enumerate(rows):
        w2 = jnp.concatenate([w_buf[row : row + BLOCK, : 2 * BLOCK] for row in pair], axis=0)
        part = lax.dot_general(grads, w2, NT, preferred_element_type=F32).astype(BF)
        for core in range(CORE):
            block = part[:, core * BLOCK : (core + 1) * BLOCK].reshape(SHARDS, share, BLOCK)
            first = (i * CORE + core) * share
            out[:, first : first + share, :] = block


def ffn(normed, cot, gain, weights):
    tokens, width = normed.shape
    rows = width // BLOCK * (tokens // SHARDS)
    vmem = pl.BlockSpec(memory_space=pltpu.VMEM)
    anyw = pl.BlockSpec(memory_space=pl.ANY)
    scale = 1.0 / math.sqrt(tokens * Z * YH * CORE)
    buffers = [pltpu.VMEM(x.shape, BF) for x in (normed, cot, weights)]
    return pl.pallas_call(
        functools.partial(ffn_kernel, scale),
        out_shape=(
            jax.ShapeDtypeStruct((SHARDS, rows, BLOCK), BF),
            jax.ShapeDtypeStruct((8, BLOCK), F32),
        ),
        in_specs=[anyw, anyw, vmem, anyw],
        out_specs=(vmem, vmem),
        scratch_shapes=buffers + [pltpu.SemaphoreType.DMA((3 * Z,))],
        compiler_params=pltpu.CompilerParams(vmem_limit_bytes=56 << 20),
        name="pruned_ffn",
    )(normed, cot, gain, weights)


def final_kernel(place, counts, act, gain, parts, units, grad, shares):
    share, width = act.shape
    x = act[...].astype(F32)
    inv = lax.rsqrt(jnp.mean(x * x, axis=-1, keepdims=True) + 1e-05)
    dnormed = []
    for j in range(width // BLOCK):
        total = parts[0, j * share : (j + 1) * share, :].astype(F32)
        for src in range(1, SHARDS):
            total += parts[src, j * share : (j + 1) * share, :].astype(F32)
        dnormed.append(total)
    scaled = jnp.concatenate(dnormed, axis=1) * gain[...].astype(F32)
    normalized = x * inv
    mean = jnp.mean(scaled * normalized, axis=-1, keepdims=True)
    grad[...] = (inv * (scaled - normalized * mean)).astype(BF)
    me = place[0]
    dp = (lax.axis_index("z") * YH + lax.axis_index("yh")) * CORE + lax.axis_index("core")
    first, count = jnp.int32(0), jnp.int32(0)
    for shard in range(SHARDS):
        first += jnp.where(shard < me, counts[shard], 0)
        count += jnp.where(shard == me, counts[shard], 0)
    lane = lax.broadcasted_iota(jnp.int32, (1, BLOCK), 1)
    wide = shares.shape[1]
    for k in range(shares.shape[0]):
        total = jnp.zeros((1, BLOCK), F32)
        for source in range(SHARDS):
            row = source % X * YL + source // X
            wanted = (source == first + k) & (k < count)
            total = jnp.where(wanted, units[row : row + 1, :], total)
        for i in range(wide):
            value = jnp.where(lane == dp * wide + i, total, 0.0)
            shares[k : k + 1, i : i + 1] = jnp.sum(value, axis=1, keepdims=True)


def final(place, counts, act, gain, parts, units):
    tokens, width = act.shape
    share = tokens // SHARDS
    wide = BLOCK // (Z * YH * CORE)
    return pl.pallas_call(
        final_kernel,
        out_shape=(
            jax.ShapeDtypeStruct((share, width), BF),
            jax.ShapeDtypeStruct((2, wide), F32),
        ),
        grid_spec=pltpu.PrefetchScalarGridSpec(
            num_scalar_prefetch=2,
            grid=(1,),
            in_specs=[
                pl.BlockSpec((share, width), lambda i, p, n: (p[0], 0)),
                pl.BlockSpec((1, width), lambda i, p, n: (0, 0)),
                pl.BlockSpec(parts.shape, lambda i, p, n: (0, 0, 0)),
                pl.BlockSpec(units.shape, lambda i, p, n: (0, 0)),
            ],
            out_specs=(
                pl.BlockSpec((share, width), lambda i, p, n: (0, 0)),
                pl.BlockSpec((2, wide), lambda i, p, n: (0, 0)),
            ),
        ),
        compiler_params=pltpu.CompilerParams(vmem_limit_bytes=12 << 20),
        name="input_grad",
    )(place, counts, act, gain.reshape(1, -1), parts, units)


def per_device(
    activations, norm_gain, gate_w, up_w, down_w, mask_gain, kept_blocks, kept_counts, cotangent
):
    me = lax.axis_index(TENSOR)
    shards = jnp.arange(SHARDS)
    blocks = mask_gain.shape[0] // BLOCK
    sent = pack(me.reshape(1), kept_blocks, kept_counts, gate_w, up_w, down_w)
    got = lax.all_to_all(sent, TENSOR, split_axis=0, concat_axis=0, tiled=True)
    ends = jnp.cumsum(kept_counts)
    source = jnp.minimum(jnp.sum((ends <= me).astype(jnp.int32)), SHARDS - 1)
    slot = lax.dynamic_index_in_dim(got, source, 0, keepdims=False)
    column = lax.all_gather(slot, "yh", axis=0, tiled=True)
    weights = lax.all_gather(column, ("z", "core"), axis=0, tiled=True)

    late, _ = lax.optimization_barrier(((cotangent, activations, mask_gain, kept_blocks, kept_counts), column))
    cotangent, act, mask_gain, kept_blocks, kept_counts = late
    kept = jnp.clip(kept_blocks[me], 0, blocks - 1)
    copies = jnp.broadcast_to(cotangent[None], (SHARDS,) + cotangent.shape)
    cot = lax.all_to_all(copies, TENSOR, split_axis=0, concat_axis=0, tiled=True)
    cot = cot.reshape(-1, cotangent.shape[1])
    act = act.astype(F32)
    inv_rms = lax.rsqrt(jnp.mean(act * act, axis=-1, keepdims=True) + 1e-05)
    normed = (act * inv_rms * norm_gain.astype(F32)).astype(BF)
    gains = jnp.take(mask_gain.reshape(blocks, BLOCK), kept, axis=0)
    gains = lax.all_gather(gains, TENSOR, axis=0, tiled=True)
    which = me - jnp.sum(jnp.where(shards == source, ends - kept_counts, 0))
    unit_gain = lax.dynamic_slice_in_dim(gains, source * 2 + jnp.clip(which, 0, 1), 1, 0)

    parts, unit = ffn(normed, cot, unit_gain, weights)
    got = lax.all_to_all(parts, TENSOR, split_axis=0, concat_axis=0, tiled=True)
    unit = unit + lax.ppermute(unit, "core", [(0, 1), (1, 0)])
    unit = jnp.sum(lax.all_gather(unit[:1], "z", axis=0, tiled=True), axis=0, keepdims=True)
    unit = lax.all_gather(unit, ("yh", "yl"), axis=0, tiled=True)
    unit = jnp.sum(unit.reshape(YH, YL, BLOCK), axis=0)
    units = lax.all_gather(unit, "x", axis=0, tiled=True)
    input_grad, gain_grad = final(me.reshape(1), kept_counts, activations, norm_gain, got, units)
    return input_grad, gain_grad


def solution(mesh):
    fine = Mesh(mesh.devices.reshape(Z, YH, CORE, YL, X), DP + TENSOR)
    placed = (
        P(DP, None),
        P(),
        P(DP, TENSOR),
        P(DP, TENSOR),
        P(TENSOR, DP),
        P(TENSOR),
        P(),
        P(),
        P(DP + TENSOR, None),
    )
    return jax.shard_map(
        per_device,
        mesh=fine,
        in_specs=placed,
        out_specs=(P(DP + TENSOR, None), P(TENSOR, DP)),
        check_vma=False,
    )
```

```python
import functools
import math

import jax
import jax.numpy as jnp
from jax import lax
from jax.experimental import pallas as pl
from jax.experimental.pallas import tpu as pltpu
from jax.sharding import Mesh
from jax.sharding import PartitionSpec as P

BLOCK = 128
Z, YH, CORE, YL, X = 8, 4, 2, 2, 4
DP = ("z", "yh", "core")
TENSOR = ("yl", "x")
SHARDS = YL * X
BF, F32 = jnp.bfloat16, jnp.float32
NT = (((1,), (1,)), ((), ()))


def pack_kernel(me, kept, counts, g0, g1, u0, u1, d0, d1, out):
    first = jnp.int32(0)
    for shard in range(SHARDS):
        first += jnp.where(shard < me[0], counts[shard], 0)
    slots = [
        jnp.concatenate([gate[...], up[...], down[...].T], axis=1)
        for gate, up, down in ((g0, u0, d0), (g1, u1, d1))
    ]
    for dest in range(SHARDS):
        out[dest] = jnp.where(dest == first + 1, slots[1], slots[0])


def pack(me, kept, counts, gate_w, up_w, down_w):
    rows, units = gate_w.shape

    def block(kept, me, k):
        return jnp.clip(kept[me[0], k], 0, units // BLOCK - 1)

    cols = [pl.BlockSpec((rows, BLOCK), lambda i, m, b, n, k=k: (0, block(b, m, k))) for k in (0, 1)]
    down = [pl.BlockSpec((BLOCK, rows), lambda i, m, b, n, k=k: (block(b, m, k), 0)) for k in (0, 1)]
    shape = (SHARDS, BLOCK, 3 * BLOCK)
    return pl.pallas_call(
        pack_kernel,
        out_shape=jax.ShapeDtypeStruct(shape, BF),
        grid_spec=pltpu.PrefetchScalarGridSpec(
            num_scalar_prefetch=3,
            grid=(1,),
            in_specs=cols + cols + down,
            out_specs=pl.BlockSpec(shape, lambda i, *_: (0, 0, 0)),
        ),
        name="pack_slots",
    )(me, kept, counts, gate_w, gate_w, up_w, up_w, down_w, down_w)


def ffn_kernel(scale, normed, cot, gain, weights, out, unit_out, n_buf, c_buf, w_buf, sems):
    chunk = normed.shape[1] // Z
    copies = []
    for i in range(Z):
        part = pl.ds(i * chunk, chunk)
        views = ((normed, n_buf, (slice(None), part)), (cot, c_buf, (slice(None), part)), (weights, w_buf, (part, slice(None))))
        for j, (source, target, at) in enumerate(views):
            one = pltpu.make_async_copy(source.at[at], target.at[at], sems.at[3 * i + j])
            one.start()
            copies.append(one)
    tokens = normed.shape[0]
    gate_up = jnp.zeros((tokens, 2 * BLOCK), F32)
    hidden = jnp.zeros((tokens, BLOCK), F32)
    rows = [
        [((z * CORE + core) * YH + yh) * BLOCK for core in range(CORE)]
        for z in range(Z) for yh in range(YH)
    ]
    wide = CORE * BLOCK
    for i, pair in enumerate(rows):
        if i % YH == 0:
            for one in copies[3 * (i // YH) : 3 * (i // YH) + 3]:
                one.wait()
        w2 = jnp.concatenate([w_buf[row : row + BLOCK, :] for row in pair], axis=0)
        gate_up += jnp.dot(n_buf[:, i * wide : (i + 1) * wide], w2[:, : 2 * BLOCK], preferred_element_type=F32)
        hidden += jnp.dot(c_buf[:, i * wide : (i + 1) * wide], w2[:, 2 * BLOCK :], preferred_element_type=F32)
    gate, up = gate_up[:, :BLOCK], gate_up[:, BLOCK:]
    sig = jax.nn.sigmoid(gate)
    unit = jnp.sum(gate * sig * up * hidden, axis=0, keepdims=True) * scale
    unit_out[...] = jnp.broadcast_to(unit, unit_out.shape)
    masked = hidden * gain[0:1, :].astype(F32)
    gate_grad = (masked * up * sig * (1.0 + gate * (1.0 - sig))).astype(BF)
    up_grad = (masked * gate * sig).astype(BF)
    grads = jnp.concatenate([gate_grad, up_grad], axis=1)
    share = tokens // SHARDS
    for i, pair in enumerate(rows):
        w2 = jnp.concatenate([w_buf[row : row + BLOCK, : 2 * BLOCK] for row in pair], axis=0)
        part = lax.dot_general(grads, w2, NT, preferred_element_type=F32).astype(BF)
        for core in range(CORE):
            block = part[:, core * BLOCK : (core + 1) * BLOCK].reshape(SHARDS, share, BLOCK)
            first = (i * CORE + core) * share
            out[:, first : first + share, :] = block


def ffn(normed, cot, gain, weights):
    tokens, width = normed.shape
    rows = width // BLOCK * (tokens // SHARDS)
    vmem = pl.BlockSpec(memory_space=pltpu.VMEM)
    anyw = pl.BlockSpec(memory_space=pl.ANY)
    scale = 1.0 / math.sqrt(tokens * Z * YH * CORE)
    buffers = [pltpu.VMEM(x.shape, BF) for x in (normed, cot, weights)]
    return pl.pallas_call(
        functools.partial(ffn_kernel, scale),
        out_shape=(
            jax.ShapeDtypeStruct((SHARDS, rows, BLOCK), BF),
            jax.ShapeDtypeStruct((8, BLOCK), F32),
        ),
        in_specs=[anyw, anyw, vmem, anyw],
        out_specs=(vmem, vmem),
        scratch_shapes=buffers + [pltpu.SemaphoreType.DMA((3 * Z,))],
        compiler_params=pltpu.CompilerParams(vmem_limit_bytes=56 << 20),
        name="pruned_ffn",
    )(normed, cot, gain, weights)


def final_kernel(place, counts, act, gain, parts, units, grad, shares):
    share, width = act.shape
    x = act[...].astype(F32)
    inv = lax.rsqrt(jnp.mean(x * x, axis=-1, keepdims=True) + 1e-05)
    dnormed = []
    for j in range(width // BLOCK):
        total = parts[0, j * share : (j + 1) * share, :].astype(F32)
        for src in range(1, SHARDS):
            total += parts[src, j * share : (j + 1) * share, :].astype(F32)
        dnormed.append(total)
    scaled = jnp.concatenate(dnormed, axis=1) * gain[...].astype(F32)
    normalized = x * inv
    mean = jnp.mean(scaled * normalized, axis=-1, keepdims=True)
    grad[...] = (inv * (scaled - normalized * mean)).astype(BF)
    me = place[0]
    dp = (lax.axis_index("z") * YH + lax.axis_index("yh")) * CORE + lax.axis_index("core")
    first, count = jnp.int32(0), jnp.int32(0)
    for shard in range(SHARDS):
        first += jnp.where(shard < me, counts[shard], 0)
        count += jnp.where(shard == me, counts[shard], 0)
    lane = lax.broadcasted_iota(jnp.int32, (1, BLOCK), 1)
    wide = shares.shape[1]
    for k in range(shares.shape[0]):
        total = jnp.zeros((1, BLOCK), F32)
        for source in range(SHARDS):
            row = source % X * YL + source // X
            wanted = (source == first + k) & (k < count)
            total = jnp.where(wanted, units[row : row + 1, :], total)
        for i in range(wide):
            value = jnp.where(lane == dp * wide + i, total, 0.0)
            shares[k : k + 1, i : i + 1] = jnp.sum(value, axis=1, keepdims=True)


def final(place, counts, act, gain, parts, units):
    tokens, width = act.shape
    share = tokens // SHARDS
    wide = BLOCK // (Z * YH * CORE)
    return pl.pallas_call(
        final_kernel,
        out_shape=(
            jax.ShapeDtypeStruct((share, width), BF),
            jax.ShapeDtypeStruct((2, wide), F32),
        ),
        grid_spec=pltpu.PrefetchScalarGridSpec(
            num_scalar_prefetch=2,
            grid=(1,),
            in_specs=[
                pl.BlockSpec((share, width), lambda i, p, n: (p[0], 0)),
                pl.BlockSpec((1, width), lambda i, p, n: (0, 0)),
                pl.BlockSpec(parts.shape, lambda i, p, n: (0, 0, 0)),
                pl.BlockSpec(units.shape, lambda i, p, n: (0, 0)),
            ],
            out_specs=(
                pl.BlockSpec((share, width), lambda i, p, n: (0, 0)),
                pl.BlockSpec((2, wide), lambda i, p, n: (0, 0)),
            ),
        ),
        compiler_params=pltpu.CompilerParams(vmem_limit_bytes=12 << 20),
        name="input_grad",
    )(place, counts, act, gain.reshape(1, -1), parts, units)


def per_device(
    activations, norm_gain, gate_w, up_w, down_w, mask_gain, kept_blocks, kept_counts, cotangent
):
    me = lax.axis_index(TENSOR)
    shards = jnp.arange(SHARDS)
    blocks = mask_gain.shape[0] // BLOCK
    sent = pack(me.reshape(1), kept_blocks, kept_counts, gate_w, up_w, down_w)
    got = lax.all_to_all(sent, TENSOR, split_axis=0, concat_axis=0, tiled=True)
    ends = jnp.cumsum(kept_counts)
    source = jnp.minimum(jnp.sum((ends <= me).astype(jnp.int32)), SHARDS - 1)
    slot = lax.dynamic_index_in_dim(got, source, 0, keepdims=False)
    column = lax.all_gather(slot, "yh", axis=0, tiled=True)
    weights = lax.all_gather(column, ("z", "core"), axis=0, tiled=True)

    late, _ = lax.optimization_barrier(((cotangent, activations, mask_gain, kept_blocks, kept_counts), column))
    cotangent, act, mask_gain, kept_blocks, kept_counts = late
    kept = jnp.clip(kept_blocks[me], 0, blocks - 1)
    copies = jnp.broadcast_to(cotangent[None], (SHARDS,) + cotangent.shape)
    cot = lax.all_to_all(copies, TENSOR, split_axis=0, concat_axis=0, tiled=True)
    cot = cot.reshape(-1, cotangent.shape[1])
    act = act.astype(F32)
    inv_rms = lax.rsqrt(jnp.mean(act * act, axis=-1, keepdims=True) + 1e-05)
    normed = (act * inv_rms * norm_gain.astype(F32)).astype(BF)
    gains = jnp.take(mask_gain.reshape(blocks, BLOCK), kept, axis=0)
    gains = lax.all_gather(gains, TENSOR, axis=0, tiled=True)
    which = me - jnp.sum(jnp.where(shards == source, ends - kept_counts, 0))
    unit_gain = lax.dynamic_slice_in_dim(gains, source * 2 + jnp.clip(which, 0, 1), 1, 0)

    parts, unit = ffn(normed, cot, unit_gain, weights)
    unit = lax.all_gather(unit[:1], ("yh", "yl"), axis=0, tiled=True)
    unit = jnp.sum(unit.reshape(YH, YL, BLOCK), axis=0)
    parts, unit = lax.optimization_barrier((parts, unit))
    got = lax.all_to_all(parts, TENSOR, split_axis=0, concat_axis=0, tiled=True)
    unit = unit + lax.ppermute(unit, "core", [(0, 1), (1, 0)])
    unit = jnp.sum(lax.all_gather(unit, "z", axis=0, tiled=True).reshape(Z, YL, BLOCK), axis=0)
    units = lax.all_gather(unit, "x", axis=0, tiled=True)
    input_grad, gain_grad = final(me.reshape(1), kept_counts, activations, norm_gain, got, units)
    return input_grad, gain_grad


def solution(mesh):
    fine = Mesh(mesh.devices.reshape(Z, YH, CORE, YL, X), DP + TENSOR)
    placed = (
        P(DP, None),
        P(),
        P(DP, TENSOR),
        P(DP, TENSOR),
        P(TENSOR, DP),
        P(TENSOR),
        P(),
        P(),
        P(DP + TENSOR, None),
    )
    return jax.shard_map(
        per_device,
        mesh=fine,
        in_specs=placed,
        out_specs=(P(DP + TENSOR, None), P(TENSOR, DP)),
        check_vma=False,
    )
```

```python
import functools
import math

import jax
import jax.numpy as jnp
from jax import lax
from jax.experimental import pallas as pl
from jax.experimental.pallas import tpu as pltpu
from jax.sharding import Mesh
from jax.sharding import PartitionSpec as P

BLOCK = 128
Z, YH, CORE, YL, X = 8, 4, 2, 2, 4
DP = ("z", "yh", "core")
TENSOR = ("yl", "x")
SHARDS = YL * X
BF, F32 = jnp.bfloat16, jnp.float32
NT = (((1,), (1,)), ((), ()))


def pack_kernel(me, kept, counts, g0, g1, u0, u1, d0, d1, out):
    first = jnp.int32(0)
    for shard in range(SHARDS):
        first += jnp.where(shard < me[0], counts[shard], 0)
    slots = [
        jnp.concatenate([gate[...], up[...], down[...].T], axis=1)
        for gate, up, down in ((g0, u0, d0), (g1, u1, d1))
    ]
    for dest in range(SHARDS):
        out[dest] = jnp.where(dest == first + 1, slots[1], slots[0])


def pack(me, kept, counts, gate_w, up_w, down_w):
    rows, units = gate_w.shape

    def block(kept, me, k):
        return jnp.clip(kept[me[0], k], 0, units // BLOCK - 1)

    cols = [pl.BlockSpec((rows, BLOCK), lambda i, m, b, n, k=k: (0, block(b, m, k))) for k in (0, 1)]
    down = [pl.BlockSpec((BLOCK, rows), lambda i, m, b, n, k=k: (block(b, m, k), 0)) for k in (0, 1)]
    shape = (SHARDS, BLOCK, 3 * BLOCK)
    return pl.pallas_call(
        pack_kernel,
        out_shape=jax.ShapeDtypeStruct(shape, BF),
        grid_spec=pltpu.PrefetchScalarGridSpec(
            num_scalar_prefetch=3,
            grid=(1,),
            in_specs=cols + cols + down,
            out_specs=pl.BlockSpec(shape, lambda i, *_: (0, 0, 0)),
        ),
        name="pack_slots",
    )(me, kept, counts, gate_w, gate_w, up_w, up_w, down_w, down_w)


def ffn_kernel(scale, normed, cot, gain, weights, out, unit_out, n_buf, c_buf, w_buf, sems):
    chunk = normed.shape[1] // Z
    copies = []
    for i in range(Z):
        part = pl.ds(i * chunk, chunk)
        views = ((normed, n_buf, (slice(None), part)), (cot, c_buf, (slice(None), part)), (weights, w_buf, (part, slice(None))))
        for j, (source, target, at) in enumerate(views):
            one = pltpu.make_async_copy(source.at[at], target.at[at], sems.at[3 * i + j])
            one.start()
            copies.append(one)
    tokens = normed.shape[0]
    gate_up = jnp.zeros((tokens, 2 * BLOCK), F32)
    hidden = jnp.zeros((tokens, BLOCK), F32)
    rows = [
        [((z * CORE + core) * YH + yh) * BLOCK for yh in range(YH) for core in range(CORE)]
        for z in range(Z)
    ]
    for i, group in enumerate(rows):
        for one in copies[3 * i : 3 * i + 3]:
            one.wait()
        w = jnp.concatenate([w_buf[row : row + BLOCK, :] for row in group], axis=0)
        cols = slice(i * chunk, (i + 1) * chunk)
        gate_up += jnp.dot(n_buf[:, cols], w[:, : 2 * BLOCK], preferred_element_type=F32)
        hidden += jnp.dot(c_buf[:, cols], w[:, 2 * BLOCK :], preferred_element_type=F32)
    gate, up = gate_up[:, :BLOCK], gate_up[:, BLOCK:]
    sig = jax.nn.sigmoid(gate)
    unit = jnp.sum(gate * sig * up * hidden, axis=0, keepdims=True) * scale
    unit_out[...] = jnp.broadcast_to(unit, unit_out.shape)
    masked = hidden * gain[0:1, :].astype(F32)
    gate_grad = (masked * up * sig * (1.0 + gate * (1.0 - sig))).astype(BF)
    up_grad = (masked * gate * sig).astype(BF)
    grads = jnp.concatenate([gate_grad, up_grad], axis=1)
    share = tokens // SHARDS
    for i, group in enumerate(rows):
        w = jnp.concatenate([w_buf[row : row + BLOCK, : 2 * BLOCK] for row in group], axis=0)
        part = lax.dot_general(grads, w, NT, preferred_element_type=F32).astype(BF)
        for j in range(len(group)):
            block = part[:, j * BLOCK : (j + 1) * BLOCK].reshape(SHARDS, share, BLOCK)
            first = (i * len(group) + j) * share
            out[:, first : first + share, :] = block


def ffn(normed, cot, gain, weights):
    tokens, width = normed.shape
    rows = width // BLOCK * (tokens // SHARDS)
    vmem = pl.BlockSpec(memory_space=pltpu.VMEM)
    anyw = pl.BlockSpec(memory_space=pl.ANY)
    scale = 1.0 / math.sqrt(tokens * Z * YH * CORE)
    buffers = [pltpu.VMEM(x.shape, BF) for x in (normed, cot, weights)]
    return pl.pallas_call(
        functools.partial(ffn_kernel, scale),
        out_shape=(
            jax.ShapeDtypeStruct((SHARDS, rows, BLOCK), BF),
            jax.ShapeDtypeStruct((8, BLOCK), F32),
        ),
        in_specs=[anyw, anyw, vmem, anyw],
        out_specs=(vmem, vmem),
        scratch_shapes=buffers + [pltpu.SemaphoreType.DMA((3 * Z,))],
        compiler_params=pltpu.CompilerParams(vmem_limit_bytes=56 << 20),
        name="pruned_ffn",
    )(normed, cot, gain, weights)


def final_kernel(place, act, gain, parts, grad):
    share, width = act.shape
    x = act[...].astype(F32)
    inv = lax.rsqrt(jnp.mean(x * x, axis=-1, keepdims=True) + 1e-05)
    dnormed = []
    for j in range(width // BLOCK):
        total = parts[0, j * share : (j + 1) * share, :].astype(F32)
        for src in range(1, SHARDS):
            total += parts[src, j * share : (j + 1) * share, :].astype(F32)
        dnormed.append(total)
    scaled = jnp.concatenate(dnormed, axis=1) * gain[...].astype(F32)
    normalized = x * inv
    mean = jnp.mean(scaled * normalized, axis=-1, keepdims=True)
    grad[...] = (inv * (scaled - normalized * mean)).astype(BF)


def final(place, act, gain, parts):
    tokens, width = act.shape
    share = tokens // SHARDS
    return pl.pallas_call(
        final_kernel,
        out_shape=jax.ShapeDtypeStruct((share, width), BF),
        grid_spec=pltpu.PrefetchScalarGridSpec(
            num_scalar_prefetch=1,
            grid=(1,),
            in_specs=[
                pl.BlockSpec((share, width), lambda i, p: (p[0], 0)),
                pl.BlockSpec((1, width), lambda i, p: (0, 0)),
                pl.BlockSpec(parts.shape, lambda i, p: (0, 0, 0)),
            ],
            out_specs=pl.BlockSpec((share, width), lambda i, p: (0, 0)),
        ),
        compiler_params=pltpu.CompilerParams(vmem_limit_bytes=12 << 20),
        name="input_grad",
    )(place, act, gain.reshape(1, -1), parts)


def per_device(
    activations, norm_gain, gate_w, up_w, down_w, mask_gain, kept_blocks, kept_counts, cotangent
):
    me = lax.axis_index(TENSOR)
    shards, k = jnp.arange(SHARDS), jnp.arange(2)
    blocks = mask_gain.shape[0] // BLOCK
    sent = pack(me.reshape(1), kept_blocks, kept_counts, gate_w, up_w, down_w)
    got = lax.all_to_all(sent, TENSOR, split_axis=0, concat_axis=0, tiled=True)
    ends = jnp.cumsum(kept_counts)
    source = jnp.minimum(jnp.sum((ends <= me).astype(jnp.int32)), SHARDS - 1)
    slot = lax.dynamic_index_in_dim(got, source, 0, keepdims=False)
    column = lax.all_gather(slot, "yh", axis=0, tiled=True)
    weights = lax.all_gather(column, ("z", "core"), axis=0, tiled=True)

    late, _ = lax.optimization_barrier(((cotangent, activations, mask_gain, kept_blocks, kept_counts), column))
    cotangent, act, mask_gain, kept_blocks, kept_counts = late
    kept = jnp.clip(kept_blocks[me], 0, blocks - 1)
    first = jnp.sum(jnp.where(shards < me, kept_counts, 0))
    copies = jnp.broadcast_to(cotangent[None], (SHARDS,) + cotangent.shape)
    cot = lax.all_to_all(copies, TENSOR, split_axis=0, concat_axis=0, tiled=True)
    cot = cot.reshape(-1, cotangent.shape[1])
    act = act.astype(F32)
    inv_rms = lax.rsqrt(jnp.mean(act * act, axis=-1, keepdims=True) + 1e-05)
    normed = (act * inv_rms * norm_gain.astype(F32)).astype(BF)
    gains = jnp.take(mask_gain.reshape(blocks, BLOCK), kept, axis=0)
    gains = lax.all_gather(gains, TENSOR, axis=0, tiled=True)
    which = me - jnp.sum(jnp.where(shards == source, ends - kept_counts, 0))
    unit_gain = lax.dynamic_slice_in_dim(gains, source * 2 + jnp.clip(which, 0, 1), 1, 0)

    parts, unit = ffn(normed, cot, unit_gain, weights)
    got = lax.all_to_all(parts, TENSOR, split_axis=0, concat_axis=0, tiled=True)
    unit = unit + lax.ppermute(unit, "core", [(0, 1), (1, 0)])
    unit = jnp.sum(lax.all_gather(unit[:1], "z", axis=0, tiled=True), axis=0)
    unit, got = lax.optimization_barrier((unit, got))
    copies = jnp.broadcast_to(unit[None, None], (YH * SHARDS, 1, BLOCK))
    units = lax.all_to_all(copies, ("yh",) + TENSOR, split_axis=0, concat_axis=0, tiled=True)
    input_grad = final(me.reshape(1), activations, norm_gain, got)
    width = BLOCK // (Z * YH * CORE)
    units = lax.dynamic_slice_in_dim(units.reshape(YH * SHARDS, BLOCK), lax.axis_index(DP) * width, width, 1)
    count = kept_counts[me]
    owner = jnp.tile(shards, YH)
    wanted = (owner[None] == first + k[:, None]) & (k < count)[:, None]
    gain_grad = jnp.sum(jnp.where(wanted[:, :, None], units[None], 0.0), axis=1)
    return input_grad, gain_grad


def solution(mesh):
    fine = Mesh(mesh.devices.reshape(Z, YH, CORE, YL, X), DP + TENSOR)
    placed = (
        P(DP, None),
        P(),
        P(DP, TENSOR),
        P(DP, TENSOR),
        P(TENSOR, DP),
        P(TENSOR),
        P(),
        P(),
        P(DP + TENSOR, None),
    )
    return jax.shard_map(
        per_device,
        mesh=fine,
        in_specs=placed,
        out_specs=(P(DP + TENSOR, None), P(TENSOR, DP)),
        check_vma=False,
    )
```
